128 devices in a mesh: call: 8 (over z, core), utt: 16 (over x, y).
Axes of the slice: x: 4, y: 4, z: 4, core: 2. Of those that a mesh axis runs over, the one named last changes fastest.
Arguments:
- queries: bfloat16 [128, 256, 1280], P(('call', 'utt')), may hold values from -300 to 300
- own_keys: bfloat16 [128, 256, 1280], P(('call', 'utt')), may hold values from -6.5 to 6.5
- own_values: bfloat16 [128, 256, 1280], P(('call', 'utt')), may hold values from -6 to 6
- lengths: int32 [128], P(('call', 'utt')), may hold values from 1 to 4, as said below
- history: int32 [128, 8], P(('call', 'utt')), may hold values from 0 to 31, as said below
- cache_blocks: bfloat16 [256, 2, 64, 1280], P(('call', 'utt')), may hold values from -6 to 6
- out_weight: bfloat16 [1280, 1280], P(('call', 'utt')), may hold values from -0.15625 to 0.15625
- grad_out: bfloat16 [128, 256, 1280], P(('call', 'utt')), may hold values from -6 to 6
Outputs:
- attended: bfloat16 [128, 256, 1280], P(('call', 'utt'))
- grad_queries: bfloat16 [128, 256, 1280], P(('call', 'utt'))
- grad_keys: bfloat16 [128, 256, 1280], P(('call', 'utt'))
- grad_values: bfloat16 [128, 256, 1280], P(('call', 'utt'))
- grad_cache: float32 [256, 2, 64, 1280], P(('call', 'utt'))
- grad_weight: float32 [1280, 1280], P(('call', 'utt'))
The draws below stay inside these ranges and needn't reach their ends.
Inputs may be any that keep to these rules, and one draw needn't show every extreme that they name: `history`: ids count within the call group: the block with id i is row i % 2 of the device at index i // 2 along utt in that group. An utterance names 8 blocks of 8 different owners; all utterances of one device that name a given owner name the same block of it. `lengths`: every device holds an utterance of 4 blocks.
All inputs are finite; a program needn't handle non-finite values.
Results may differ from the reference program's by a relative error of at most 0.014.
Values may be sent and summed in bfloat16 or wider, within the bound.
No kernel may reach another device: no remote copies, remote signals or barrier semaphores. Data moves between devices by JAX's collectives and lax.ppermute only.
A program may use at most 128 MiB of HBM per device.

```python
import jax
import jax.numpy as jnp
from jax import lax

D = 1280
HEADS = 20
HD = 64
BLK = 64
LB = 4
HIST = 8
UTT_DEV = 1
CB_DEV = 2
FR = 256
UTTS = 128
CBLK = 256
N_UTT = 16


def common_base(key):
    return jnp.clip(jax.random.normal(key, (UTTS, FR, D), jnp.float32), -6.0, 6.0)


def draw_own_keys(key, part):
    base = common_base(key)
    return base.astype(jnp.bfloat16)


def draw_queries(key, part):
    key = jax.random.fold_in(key, 5)
    fresh = jnp.clip(jax.random.normal(key, (UTTS, FR, D), jnp.float32), -6.0, 6.0)
    return fresh.astype(jnp.bfloat16)


def draw_history(key, part):
    key = jax.random.fold_in(key, 7)
    device_count = UTTS // UTT_DEV

    def one_device(dev_key):
        local_key, owner_key = jax.random.split(dev_key)
        local_rows = jax.random.randint(local_key, (N_UTT,), 0, CB_DEV, dtype=jnp.int32)
        block_ids = jnp.arange(N_UTT, dtype=jnp.int32) * CB_DEV + local_rows

        def pick(pick_key):
            return jax.random.permutation(pick_key, N_UTT)[:HIST]
        owners = jax.vmap(pick)(jax.random.split(owner_key, UTT_DEV))
        return block_ids[owners]
    rows = jax.vmap(one_device)(jax.random.split(key, device_count))
    return rows.reshape(UTTS, HIST).astype(jnp.int32)


def draw_lengths(key, part):
    key = jax.random.fold_in(key, 9)
    device_count = UTTS // UTT_DEV
    first_key, second_key = jax.random.split(key)
    drawn = jax.random.randint(first_key, (device_count, UTT_DEV), 1, LB + 1, dtype=jnp.int32)
    longest = jax.random.randint(second_key, (device_count, 1), 0, UTT_DEV, dtype=jnp.int32)
    places = jnp.arange(UTT_DEV, dtype=jnp.int32)[None, :]
    drawn = jnp.where(places == longest, LB, drawn)
    return drawn.reshape(UTTS).astype(jnp.int32)


def shard_levels(stream_key, shape, shards, smallest, high):
    gain, own = 1.0, jax.random.fold_in(stream_key, 6)
    for position, blocks in shards:
        steps = jnp.exp(jax.random.uniform(jax.random.fold_in(own, position), (blocks,), jnp.float32, smallest / len(shards), high / len(shards)))
        gain = gain * jnp.repeat(steps, shape[position] // blocks).reshape([-1 if axis == position else 1 for axis in range(len(shape))])
    return gain


def centred(stream_key, shape, deviation, limit, shards=(), kind=jnp.bfloat16):
    values = deviation * jax.random.normal(stream_key, shape, jnp.float32)
    if shards:
        values = values * shard_levels(stream_key, shape, shards, -0.22, 0.18)
    return jnp.clip(values, -limit, limit).astype(kind)


def setup_inputs(seed: int = 0) -> dict:
    splits = jax.random.split(jax.random.key(seed), 9)
    queries = draw_queries(jax.random.fold_in(splits[8], 71), 0)
    own_keys = draw_own_keys(jax.random.fold_in(splits[8], 71), 0)
    own_values = centred(splits[2], (UTTS, FR, D), 1.0, 6.0, ((0, 128),))
    lengths = draw_lengths(jax.random.fold_in(splits[8], 71), 0)
    history = draw_history(jax.random.fold_in(splits[8], 71), 0)
    cache_blocks = centred(splits[5], (CBLK, 2, BLK, D), 1.0, 6.0, ((0, 128),))
    out_weight = centred(splits[6], (D, D), D ** -0.5, 0.15625, ((0, 128),))
    grad_out = centred(splits[7], (UTTS, FR, D), 1.0, 6.0, ((0, 128),))
    return {"queries": queries, "own_keys": own_keys, "own_values": own_values, "lengths": lengths, "history": history, "cache_blocks": cache_blocks, "out_weight": out_weight, "grad_out": grad_out}


def utterance_pass(query_rows, key_rows, value_rows, length, blocks, grad_rows, weight_full):
    score_scale = HD ** -0.5
    frame_ids = jnp.arange(FR, dtype=jnp.int32)
    valid = frame_ids < length * BLK
    key_all = jnp.concatenate([key_rows, blocks[:, 0].reshape(HIST * BLK, D)], 0)
    value_all = jnp.concatenate([value_rows, blocks[:, 1].reshape(HIST * BLK, D)], 0)
    key_valid = jnp.concatenate([valid, jnp.ones((HIST * BLK,), dtype=bool)], 0)
    query_heads = query_rows.astype(jnp.float32).reshape(FR, HEADS, HD)
    key_heads = key_all.astype(jnp.float32).reshape(-1, HEADS, HD)
    value_heads = value_all.astype(jnp.float32).reshape(-1, HEADS, HD)
    scores = jnp.einsum('qhd,khd->hqk', query_heads, key_heads) * score_scale
    scores = jnp.where(key_valid[None, None, :], scores, -1e30)
    top = jnp.max(scores, axis=-1, keepdims=True)
    expo = jnp.exp(scores - top)
    probs = expo / jnp.sum(expo, axis=-1, keepdims=True)
    probs_b = probs.astype(jnp.bfloat16)
    outputs = jnp.einsum('hqk,khd->qhd', probs_b.astype(jnp.float32), value_heads).reshape(FR, D)
    attn = (outputs * valid[:, None]).astype(jnp.bfloat16)
    grad_attn = (jnp.dot(grad_rows, weight_full.T, preferred_element_type=jnp.float32) * valid[:, None]).astype(jnp.bfloat16)
    grad_heads = grad_attn.astype(jnp.float32).reshape(FR, HEADS, HD)
    grad_probs = jnp.einsum('qhd,khd->hqk', grad_heads, value_heads)
    row_dots = jnp.sum(probs * grad_probs, axis=-1, keepdims=True)
    grad_scores = (probs * (grad_probs - row_dots) * score_scale).astype(jnp.bfloat16)
    grad_scores_f = grad_scores.astype(jnp.float32)
    grad_query = jnp.einsum('hqk,khd->qhd', grad_scores_f, key_heads).reshape(FR, D).astype(jnp.bfloat16)
    grad_key_all = jnp.einsum('hqk,qhd->khd', grad_scores_f, query_heads).reshape(-1, D).astype(jnp.bfloat16)
    grad_value_all = jnp.einsum('hqk,qhd->khd', probs_b.astype(jnp.float32), grad_heads).reshape(-1, D).astype(jnp.bfloat16)
    block_grads = jnp.stack([grad_key_all[FR:].reshape(HIST, BLK, D), grad_value_all[FR:].reshape(HIST, BLK, D)], 1)
    return attn, grad_query, grad_key_all[:FR], grad_value_all[:FR], block_grads


def reference(queries, own_keys, own_values, lengths, history, cache_blocks, out_weight, grad_out):
    device_count = UTTS // UTT_DEV
    group_blocks = CB_DEV * N_UTT

    def device_step(grad_cache, device):
        def take_rows(array):
            return lax.dynamic_slice_in_dim(array, (device * UTT_DEV).astype(jnp.int32), UTT_DEV, 0)

        hist_rows = take_rows(history)
        group_base = ((device // N_UTT) * group_blocks).astype(jnp.int32)
        blocks = cache_blocks[group_base + hist_rows]
        results = jax.vmap(utterance_pass, in_axes=(0, 0, 0, 0, 0, 0, None))(
            take_rows(queries), take_rows(own_keys), take_rows(own_values), take_rows(lengths),
            blocks, take_rows(grad_out), out_weight)
        attn, grad_query, grad_key, grad_value, block_grads = results
        flat_ids = hist_rows.reshape(-1)
        owner_of = flat_ids // CB_DEV
        onehot = (owner_of[None, :] == jnp.arange(N_UTT, dtype=jnp.int32)[:, None])
        slot_grad = jnp.dot(onehot.astype(jnp.float32), block_grads.reshape(UTT_DEV * HIST, -1).astype(jnp.float32)).astype(jnp.bfloat16)
        slot_ids = jnp.max(jnp.where(onehot, flat_ids[None, :], 0), axis=1).astype(jnp.int32)
        grad_cache = grad_cache.at[group_base + slot_ids].add(slot_grad.astype(jnp.float32).reshape(N_UTT, 2, BLK, D))
        return grad_cache, (attn, grad_query, grad_key, grad_value)

    start_cache = jnp.zeros((CBLK, 2, BLK, D), jnp.float32)
    grad_cache, stacked = lax.scan(device_step, start_cache, jnp.arange(device_count, dtype=jnp.int32))
    attn, grad_query, grad_key, grad_value = [x.reshape(UTTS, FR, D) for x in stacked]
    attn_flat = attn.reshape(-1, D)
    grad_flat = grad_out.reshape(-1, D)
    attended = jnp.dot(attn_flat, out_weight, preferred_element_type=jnp.float32).astype(jnp.bfloat16).reshape(UTTS, FR, D)
    grad_weight = jnp.dot(attn_flat.T, grad_flat, preferred_element_type=jnp.float32)
    return attended, grad_query, grad_key, grad_value, grad_cache, grad_weight
```

```python
import functools

import jax
import jax.numpy as jnp
from jax import lax
from jax.experimental import pallas as pl
from jax.experimental.pallas import tpu as pltpu
from jax.sharding import Mesh
from jax.sharding import PartitionSpec as P

HD = 64
BLK = 64
LANES = 128
LOG2E = 1.4426950408889634
BF = jnp.bfloat16
F32 = jnp.float32
VMEM_LIMIT = 48 * 1024 * 1024
CHUNKS = ((0, 640, "x", "y"), (640, 640, "y", "x"))


def shift(array, axis, amount):
    n = lax.axis_size(axis)
    return lax.ppermute(array, axis, [(i, (i + amount) % n) for i in range(n)])


def nt(a, b):
    return lax.dot_general(a, b, (((1,), (1,)), ((), ())), preferred_element_type=F32)


def mm(a, b):
    return lax.dot_general(a, b, (((1,), (0,)), ((), ())), preferred_element_type=F32)


def select_kernel(table, *refs):
    held, out = refs[:4], refs[4:]
    for j in range(4):
        for k in range(4):
            row = jnp.maximum(table[j * 4 + k], 0)
            out[j][k] = held[k][row]


def select_rows(table, held):
    _, kinds, rows, width = held[0].shape
    block_in = pl.BlockSpec((2, kinds, rows, LANES), lambda i, t: (0, 0, 0, i))
    block_out = pl.BlockSpec((4, kinds, rows, LANES), lambda i, t: (0, 0, 0, i))
    return pl.pallas_call(
        select_kernel,
        grid_spec=pltpu.PrefetchScalarGridSpec(
            num_scalar_prefetch=1,
            grid=(width // LANES,),
            in_specs=[block_in] * 4,
            out_specs=[block_out] * 4,
        ),
        out_shape=[jax.ShapeDtypeStruct((4, kinds, rows, width), BF)] * 4,
        compiler_params=pltpu.CompilerParams(vmem_limit_bytes=VMEM_LIMIT),
        cost_estimate=pl.CostEstimate(
            flops=0, bytes_accessed=6 * 2 * 2 * kinds * rows * width * 2, transcendentals=0
        ),
        name="select_rows",
    )(table.reshape(-1), *held)


def fold_kernel(table, *refs):
    parts, out = refs[:4], refs[4:]
    for k in range(4):
        for row in range(2):
            total = None
            for j in range(4):
                keep = jnp.where(table[j * 4 + k] == row, 1.0, 0.0).astype(F32)
                term = parts[j][k].astype(F32) * keep
                total = term if total is None else total + term
            out[k][row] = total.astype(BF)


def fold_rows(table, parts):
    _, kinds, rows, width = parts[0].shape
    block_in = pl.BlockSpec((4, kinds, rows, LANES), lambda i, t: (0, 0, 0, i))
    block_out = pl.BlockSpec((2, kinds, rows, LANES), lambda i, t: (0, 0, 0, i))
    return pl.pallas_call(
        fold_kernel,
        grid_spec=pltpu.PrefetchScalarGridSpec(
            num_scalar_prefetch=1,
            grid=(width // LANES,),
            in_specs=[block_in] * 4,
            out_specs=[block_out] * 4,
        ),
        out_shape=[jax.ShapeDtypeStruct((2, kinds, rows, width), BF)] * 4,
        compiler_params=pltpu.CompilerParams(vmem_limit_bytes=VMEM_LIMIT),
        cost_estimate=pl.CostEstimate(
            flops=0, bytes_accessed=6 * 2 * 2 * kinds * rows * width * 2, transcendentals=0
        ),
        name="fold_rows",
    )(table.reshape(-1), *parts)


def total_kernel(*refs):
    out = refs[-1]
    step = pl.program_id(0)
    start = 0
    for chunk, (_, width, _, _) in enumerate(CHUNKS):
        parts = refs[4 * chunk : 4 * chunk + 4]
        count = width // LANES

        @pl.when((step >= start) & (step < start + count))
        def _():
            total = parts[0][...].astype(F32)
            for part in parts[1:]:
                total = total + part[...].astype(F32)
            out[...] = total

        start += count


def total_rows(parts):
    owned, kinds, rows, _ = parts[0][0].shape
    specs, start = [], 0
    for _, width, _, _ in CHUNKS:
        count = width // LANES
        spec = pl.BlockSpec(
            (owned, kinds, rows, LANES),
            lambda i, start=start, count=count: (0, 0, 0, jnp.clip(i - start, 0, count - 1)),
        )
        specs += [spec] * 4
        start += count
    width = start * LANES
    return pl.pallas_call(
        total_kernel,
        grid=(start,),
        in_specs=specs,
        out_specs=pl.BlockSpec((owned, kinds, rows, LANES), lambda i: (0, 0, 0, i)),
        out_shape=jax.ShapeDtypeStruct((owned, kinds, rows, width), F32),
        compiler_params=pltpu.CompilerParams(vmem_limit_bytes=VMEM_LIMIT),
        cost_estimate=pl.CostEstimate(
            flops=0, bytes_accessed=owned * kinds * rows * width * 12, transcendentals=0
        ),
        name="total_rows",
    )(*[part for group in parts for part in group])


def attend_kernel(meta, *refs):
    q_ref, ko_ref, vo_ref, g_ref, s0, s1, s2, s3 = refs[:8]
    slots = (s0, s1, s2, s3)
    attn_ref, attn_t_ref, dq_ref, dk_ref, dv_ref, t0, t1, t2, t3, k_all, v_all = refs[-11:]
    back = (t0, t1, t2, t3)
    frames = q_ref.shape[0]
    entries = (k_all.shape[0] - frames) // BLK
    k_all[:frames] = ko_ref[...]
    v_all[:frames] = vo_ref[...]
    for i in range(entries):
        place = pl.ds(frames + BLK * i, BLK)
        for j in range(4):

            @pl.when(meta[i] == j)
            def _():
                k_all[place] = slots[j][meta[entries + i], 0]
                v_all[place] = slots[j][meta[entries + i], 1]

    keys, values = k_all[...], v_all[...]
    query, grad = q_ref[...], g_ref[...]
    keys_t, values_t = keys.T, values.T
    count = keys.shape[0]
    valid_frames = meta[2 * entries] * BLK
    lane = lax.broadcasted_iota(jnp.int32, query.shape, 1)
    key_row = lax.broadcasted_iota(jnp.int32, (frames, frames), 0)
    outs_t, dqs_t = [], []
    grad_key = grad_value = None
    for h in range(2):
        mine = (lane >= h * HD) & (lane < (h + 1) * HD)
        query_h = jnp.where(mine, query, jnp.zeros_like(query))
        grad_h = jnp.where(mine, grad, jnp.zeros_like(grad))
        scores = nt(keys, query_h)
        scores = jnp.concatenate(
            [jnp.where(key_row < valid_frames, scores[:frames], -1e30), scores[frames:]], 0
        )
        top = jnp.max(scores, axis=0, keepdims=True)
        expo = jnp.exp2((scores - top) * (HD**-0.5 * LOG2E))
        inverse = 1.0 / jnp.sum(expo, axis=0, keepdims=True)
        probs = expo * inverse
        probs_b = probs.astype(BF)
        grad_probs = nt(values, grad_h)
        row_dots = jnp.sum(probs * grad_probs, axis=0, keepdims=True)
        grad_scores = (probs * (grad_probs - row_dots) * HD**-0.5).astype(BF)
        outs_t.append(mm(values_t[h * HD : (h + 1) * HD], probs_b))
        dqs_t.append(mm(keys_t[h * HD : (h + 1) * HD], grad_scores))
        part_key = mm(grad_scores, query_h)
        part_value = mm(probs_b, grad_h)
        grad_key = part_key if grad_key is None else grad_key + part_key
        grad_value = part_value if grad_value is None else grad_value + part_value
    out_t = jnp.concatenate(outs_t, 0)
    column = lax.broadcasted_iota(jnp.int32, out_t.shape, 1)
    out_t = jnp.where(column < valid_frames, out_t, 0.0)
    attn_t_ref[...] = out_t.astype(BF)
    attn_ref[...] = out_t.T.astype(BF)
    dq_ref[...] = jnp.concatenate(dqs_t, 0).T.astype(BF)
    grad_key = grad_key.astype(BF)
    grad_value = grad_value.astype(BF)
    dk_ref[...] = grad_key[:frames]
    dv_ref[...] = grad_value[:frames]
    for ref in back:
        ref[...] = jnp.zeros_like(ref)
    for i in range(entries):
        rows = slice(frames + BLK * i, frames + BLK * (i + 1))
        for j in range(4):

            @pl.when(meta[i] == j)
            def _():
                back[j][meta[entries + i], 0] = grad_key[rows]
                back[j][meta[entries + i], 1] = grad_value[rows]


def attend(meta, query, own_keys, own_values, grad_attn, slots, chunk, previous):
    start, width, _, _ = chunk
    frames, features = query.shape
    entries = (meta.shape[0] - 1) // 2
    first = start // LANES
    wide = pl.BlockSpec((frames, LANES), lambda i, m: (0, first + i))
    tall = pl.BlockSpec((LANES, frames), lambda i, m: (first + i, 0))
    slot = pl.BlockSpec((4, 2, BLK, LANES), lambda i, m: (0, 0, 0, i))
    kept = list(previous or [])
    rows = jax.ShapeDtypeStruct((frames, features), BF)
    keys = frames + entries * BLK
    return pl.pallas_call(
        attend_kernel,
        grid_spec=pltpu.PrefetchScalarGridSpec(
            num_scalar_prefetch=1,
            grid=(width // LANES,),
            in_specs=[wide] * 4 + [slot] * 4 + [pl.BlockSpec(memory_space=pl.ANY)] * len(kept),
            out_specs=[wide, tall, wide, wide, wide] + [slot] * 4,
            scratch_shapes=[pltpu.VMEM((keys, LANES), BF), pltpu.VMEM((keys, LANES), BF)],
        ),
        out_shape=[rows, jax.ShapeDtypeStruct((features, frames), BF), rows, rows, rows]
        + [jax.ShapeDtypeStruct((4, 2, BLK, width), BF)] * 4,
        input_output_aliases={9 + i: i for i in range(len(kept))},
        compiler_params=pltpu.CompilerParams(vmem_limit_bytes=VMEM_LIMIT),
        cost_estimate=pl.CostEstimate(
            flops=12 * frames * keys * width,
            bytes_accessed=(9 * frames + 4 * keys) * width * 2,
            transcendentals=frames * keys * width // HD,
        ),
        name="attend",
    )(meta, query, own_keys, own_values, grad_attn, *slots, *kept)


def place_kernel(where, *refs):
    pieces, out = refs[:8], refs[8]
    for i, piece in enumerate(pieces):
        out[where[i]] = piece[...]


def spread_slabs(rows, ids):
    size, features = rows.shape
    note = jnp.pad(ids.astype(BF), (0, features - ids.shape[0]))[None]
    slab = jnp.concatenate([rows, note, jnp.zeros((15 - size, features), BF)], 0)
    row = jnp.stack([slab] + [shift(slab, "y", k) for k in range(1, 4)])
    return [row] + [shift(row, "x", k) for k in range(1, 4)]


def gather_weight(slabs, size):
    x, y, z, core = (lax.axis_index(axis) for axis in ("x", "y", "z", "core"))
    steps = jnp.arange(4, dtype=jnp.int32)
    features = slabs[0].shape[-1]
    rows = jnp.stack(slabs)[:, :, :size]
    rows = jnp.take(jnp.take(rows, (x - steps) % 4, axis=0), (y - steps) % 4, axis=1)
    rows = rows.reshape(16 * size, features)
    pieces = [rows] + [shift(rows, "z", k) for k in range(1, 4)]
    pieces += [shift(piece, "core", 1) for piece in pieces]
    from_z = (z - steps) % 4
    where = jnp.concatenate([from_z * 2 + core, from_z * 2 + 1 - core])
    wide = 2 * LANES
    weight = pl.pallas_call(
        place_kernel,
        grid_spec=pltpu.PrefetchScalarGridSpec(
            num_scalar_prefetch=1,
            grid=(features // wide,),
            in_specs=[pl.BlockSpec((16 * size, wide), lambda i, w: (0, i))] * 8,
            out_specs=pl.BlockSpec((8, 16 * size, wide), lambda i, w: (0, 0, i)),
        ),
        out_shape=jax.ShapeDtypeStruct((8, 16 * size, features), BF),
        compiler_params=pltpu.CompilerParams(vmem_limit_bytes=VMEM_LIMIT),
        cost_estimate=pl.CostEstimate(
            flops=0, bytes_accessed=2 * 8 * 16 * size * features * 2, transcendentals=0
        ),
        name="place_weight",
    )(where, *pieces)
    return weight.reshape(128 * size, features)


def grad_weight_kernel(core, attn_t_ref, grad_ref, far_ref, near_ref):
    step = pl.program_id(0)
    part = mm(attn_t_ref[...], grad_ref[...])

    @pl.when(step < 4)
    def _():
        far_ref[0] = part.astype(BF)

    @pl.when(step >= 4)
    def _():
        near_ref[0] = part


def grad_weight_rows(attn_t, grad_rows):
    features, frames = attn_t.shape
    size = features // 8
    core, z = lax.axis_index("core"), lax.axis_index("z")
    far, near = pl.pallas_call(
        grad_weight_kernel,
        grid_spec=pltpu.PrefetchScalarGridSpec(
            num_scalar_prefetch=1,
            grid=(8,),
            in_specs=[
                pl.BlockSpec(
                    (size, frames),
                    lambda i, c: (jnp.where(i < 4, 2 * i + 1 - c[0], 2 * (i - 4) + c[0]), 0),
                ),
                pl.BlockSpec((frames, features), lambda i, c: (0, 0)),
            ],
            out_specs=[
                pl.BlockSpec((1, size, features), lambda i, c: (jnp.minimum(i, 3), 0, 0)),
                pl.BlockSpec((1, size, features), lambda i, c: (jnp.maximum(i - 4, 0), 0, 0)),
            ],
        ),
        out_shape=[
            jax.ShapeDtypeStruct((4, size, features), BF),
            jax.ShapeDtypeStruct((4, size, features), F32),
        ],
        compiler_params=pltpu.CompilerParams(vmem_limit_bytes=VMEM_LIMIT),
        cost_estimate=pl.CostEstimate(
            flops=2 * features * features * frames,
            bytes_accessed=features * features * 3 + features * frames * 4,
            transcendentals=0,
        ),
        name="grad_weight",
    )(core.reshape(1).astype(jnp.int32), attn_t, grad_rows)
    total = near + shift(far, "core", 1).astype(F32)
    for axis in ("z", "x", "y"):
        me = lax.axis_index(axis)
        mine = lax.dynamic_index_in_dim(total, me, 0, keepdims=False)
        for k in range(1, 4):
            piece = lax.dynamic_index_in_dim(total, (me + k) % 4, 0, keepdims=False)
            mine = mine + shift(piece.astype(BF), axis, k).astype(F32)
        if axis == "z":
            total = mine.reshape(4, 4, size // 16, features)
        else:
            total = mine
    return total


def body(queries, own_keys, own_values, lengths, history, cache_blocks, out_weight, grad_out):
    owned = cache_blocks.shape[0]
    _, frames, features = queries.shape
    here = {axis: lax.axis_index(axis) for axis in ("x", "y")}
    ids = history[0]
    owners = ids // owned
    offset = {"x": (here["x"] - owners // 4) % 4, "y": (here["y"] - owners % 4) % 4}

    slabs = spread_slabs(out_weight, ids)
    noted = {
        "y": [ids] + [slabs[0][4 - j, out_weight.shape[0], : ids.shape[0]] for j in range(1, 4)],
        "x": [ids] + [slabs[4 - j][0, out_weight.shape[0], : ids.shape[0]] for j in range(1, 4)],
    }
    tables = {}
    for first, second in (("x", "y"), ("y", "x")):
        asked = jnp.stack([n.astype(jnp.int32) for n in noted[second]])
        along = (here[first] - jnp.arange(4, dtype=jnp.int32)) % 4
        owner = along * 4 + here["y"] if first == "x" else here["x"] * 4 + along
        match = (asked // owned)[:, None, :] == owner[None, :, None]
        tables[first] = jnp.max(jnp.where(match, (asked % owned)[:, None, :], -1), axis=2)
    weight = gather_weight(slabs, out_weight.shape[0])
    valid = (jnp.arange(frames, dtype=jnp.int32) < lengths[0] * BLK)[:, None]
    grad_attn = (nt(grad_out[0], weight) * valid).astype(BF)

    results, returned = None, []
    fetched = []
    for start, width, first, second in CHUNKS:
        part = lax.slice_in_dim(cache_blocks, start, start + width, axis=3)
        held = [part] + [shift(part, first, k) for k in range(1, 4)]
        sent = select_rows(tables[first], held)
        fetched.append([sent[0]] + [shift(sent[j], second, j) for j in range(1, 4)])
    for chunk, slots in zip(CHUNKS, fetched):
        _, _, first, second = chunk
        meta = jnp.concatenate([offset[second], offset[first], lengths]).astype(jnp.int32)
        out = attend(
            meta, queries[0], own_keys[0], own_values[0], grad_attn, slots, chunk, results
        )
        results, back = out[:5], out[5:]
        parts = [back[0]] + [shift(back[j], second, -j) for j in range(1, 4)]
        sums = fold_rows(tables[first], parts)
        returned.append([sums[0]] + [shift(sums[k], first, -k) for k in range(1, 4)])
    attn, attn_t, grad_queries, grad_keys, grad_values = results
    grad_cache = total_rows(returned)
    attended = mm(attn, weight).astype(BF)
    grad_weight = grad_weight_rows(attn_t, grad_out[0])
    return (
        attended[None],
        grad_queries[None],
        grad_keys[None],
        grad_values[None],
        grad_cache,
        grad_weight,
    )


def solution(mesh):
    axes = ("z", "core", "x", "y")
    fine = Mesh(mesh.devices.reshape(4, 2, 4, 4), axes)

    def split(rank):
        return P(axes, *([None] * (rank - 1)))

    return jax.shard_map(
        body,
        mesh=fine,
        in_specs=tuple(split(rank) for rank in (3, 3, 3, 1, 2, 4, 2, 3)),
        out_specs=tuple(split(rank) for rank in (3, 3, 3, 3, 4, 2)),
        check_vma=False,
    )
```

```python
import functools

import jax
import jax.numpy as jnp
from jax import lax
from jax.experimental import pallas as pl
from jax.experimental.pallas import tpu as pltpu
from jax.sharding import Mesh
from jax.sharding import PartitionSpec as P

HD = 64
BLK = 64
LANES = 128
LOG2E = 1.4426950408889634
BF = jnp.bfloat16
F32 = jnp.float32
MIB = 1024 * 1024
CHUNKS = ((0, 1280),)
PARTS = (((0, 1280),),)
PLANE = ("core", "x", "y")


def shift(array, axis, amount):
    n = lax.axis_size(axis)
    return lax.ppermute(array, axis, [(i, (i + amount) % n) for i in range(n)])


def move(array, leg, amount):
    pairs = []
    for core in range(2):
        for x in range(4):
            for y in range(4):
                along_x = (leg == 0) == (core == 0)
                to_x, to_y = ((x + amount) % 4, y) if along_x else (x, (y + amount) % 4)
                pairs.append((core * 16 + x * 4 + y, core * 16 + to_x * 4 + to_y))
    return lax.ppermute(array, PLANE, pairs)


def cost(us):
    return pl.CostEstimate(flops=int(us * 1.15e9), bytes_accessed=0, transcendentals=0)


def after(array, *earlier):
    return lax.optimization_barrier((array, earlier))[0]


def nt(a, b):
    return lax.dot_general(a, b, (((1,), (1,)), ((), ())), preferred_element_type=F32)


def mm(a, b):
    return lax.dot_general(a, b, (((1,), (0,)), ((), ())), preferred_element_type=F32)


def select_kernel(table, *refs):
    held, out = refs[:4], refs[4:]
    for j in range(4):
        for k in range(4):
            row = jnp.maximum(table[j * 4 + k], 0)
            out[j][k] = held[k][row]


def select_rows(table, held):
    _, kinds, rows, width = held[0].shape
    block_in = pl.BlockSpec((2, kinds, rows, LANES), lambda i, t: (0, 0, 0, i))
    block_out = pl.BlockSpec((4, kinds, rows, LANES), lambda i, t: (0, 0, 0, i))
    return pl.pallas_call(
        select_kernel,
        grid_spec=pltpu.PrefetchScalarGridSpec(
            num_scalar_prefetch=1,
            grid=(width // LANES,),
            in_specs=[block_in] * 4,
            out_specs=[block_out] * 4,
        ),
        out_shape=[jax.ShapeDtypeStruct((4, kinds, rows, width), BF)] * 4,
        compiler_params=pltpu.CompilerParams(vmem_limit_bytes=12 * MIB),
        cost_estimate=cost(3),
        name="select_rows",
    )(table.reshape(-1), *held)


def fold_kernel(table, *refs):
    parts, out = refs[:4], refs[4:]
    for k in range(4):
        for row in range(2):
            total = None
            for j in range(4):
                keep = jnp.where(table[j * 4 + k] == row, 1.0, 0.0).astype(F32)
                term = parts[j][k].astype(F32) * keep
                total = term if total is None else total + term
            out[k][row] = total.astype(BF)


def fold_rows(table, parts):
    _, kinds, rows, width = parts[0].shape
    block_in = pl.BlockSpec((4, kinds, rows, LANES), lambda i, t: (0, 0, 0, i))
    block_out = pl.BlockSpec((2, kinds, rows, LANES), lambda i, t: (0, 0, 0, i))
    return pl.pallas_call(
        fold_kernel,
        grid_spec=pltpu.PrefetchScalarGridSpec(
            num_scalar_prefetch=1,
            grid=(width // LANES,),
            in_specs=[block_in] * 4,
            out_specs=[block_out] * 4,
        ),
        out_shape=[jax.ShapeDtypeStruct((2, kinds, rows, width), BF)] * 4,
        compiler_params=pltpu.CompilerParams(vmem_limit_bytes=12 * MIB),
        cost_estimate=cost(4.5),
        name="fold_rows",
    )(table.reshape(-1), *parts)


def total_kernel(*refs):
    out = refs[-1]
    step = pl.program_id(0)
    start = 0
    for chunk, (_, width) in enumerate(CHUNKS):
        parts = refs[4 * chunk : 4 * chunk + 4]
        count = width // LANES

        @pl.when((step >= start) & (step < start + count))
        def _():
            total = parts[0][...].astype(F32)
            for part in parts[1:]:
                total = total + part[...].astype(F32)
            out[...] = total

        start += count


def total_rows(parts):
    owned, kinds, rows, _ = parts[0][0].shape
    specs, start = [], 0
    for _, width in CHUNKS:
        count = width // LANES
        spec = pl.BlockSpec(
            (owned, kinds, rows, LANES),
            lambda i, start=start, count=count: (0, 0, 0, jnp.clip(i - start, 0, count - 1)),
        )
        specs += [spec] * 4
        start += count
    width = start * LANES
    return pl.pallas_call(
        total_kernel,
        grid=(start,),
        in_specs=specs,
        out_specs=pl.BlockSpec((owned, kinds, rows, LANES), lambda i: (0, 0, 0, i)),
        out_shape=jax.ShapeDtypeStruct((owned, kinds, rows, width), F32),
        compiler_params=pltpu.CompilerParams(vmem_limit_bytes=12 * MIB),
        cost_estimate=cost(4),
        name="total_rows",
    )(*[part for group in parts for part in group])


def head_front(keys, values, query, grad_t, head):
    lane = lax.broadcasted_iota(jnp.int32, query.shape, 1) // HD
    feature = lax.broadcasted_iota(jnp.int32, grad_t.shape, 0) // HD
    query = jnp.where(lane == head, query, jnp.zeros_like(query))
    grad_t = jnp.where(feature == head, grad_t, jnp.zeros_like(grad_t))
    return query, grad_t, nt(keys, query), mm(values, grad_t)


def head_softmax(scores, grad_probs, valid_frames):
    frames = scores.shape[1]
    key_row = lax.broadcasted_iota(jnp.int32, (frames, frames), 0)
    own = jnp.where(key_row < valid_frames, scores[:frames], -1e30)
    scores = jnp.concatenate([own, scores[frames:]], 0)
    top = jnp.max(scores, axis=0, keepdims=True)
    expo = jnp.exp2((scores - top) * (HD**-0.5 * LOG2E))
    probs = expo * (1.0 / jnp.sum(expo, axis=0, keepdims=True))
    row_dots = jnp.sum(probs * grad_probs, axis=0, keepdims=True)
    return probs.astype(BF), (probs * (grad_probs - row_dots)).astype(BF)


def attend_kernel(meta, q_ref, ko_ref, vo_ref, g_ref, *refs):
    slots = refs[:4]
    attn_t_ref, dq_ref, dk_ref, dv_ref = refs[-12:-8]
    back, (k_all, v_all, dk_all, dv_all) = refs[-8:-4], refs[-4:]
    frames, width = q_ref.shape
    scale = HD**-0.5
    valid_frames = meta[16] * BLK
    k_all[:frames] = ko_ref[...]
    v_all[:frames] = vo_ref[...]

    def rows_of(place):
        return pl.ds(pl.multiple_of(frames + BLK * jnp.maximum(place, 0), BLK), BLK)

    for j in range(4):
        for k in range(4):
            place = meta[4 * j + k]

            @pl.when(place >= 0)
            def _():
                k_all[rows_of(place)] = slots[j][k, 0]
                v_all[rows_of(place)] = slots[j][k, 1]

    for pair in range(width // LANES):
        lanes = slice(pair * LANES, (pair + 1) * LANES)
        keys, values = k_all[:, lanes], v_all[:, lanes]
        keys_t, values_t = keys.T, values.T
        fronts = [head_front(keys, values, q_ref[:, lanes], g_ref[lanes], h) for h in range(2)]
        outs_t, dqs_t, dks, dvs = [], [], [], []
        for h, (query, grad_t, scores, grad_probs) in enumerate(fronts):
            probs, grad_scores = head_softmax(scores, grad_probs, valid_frames)
            mine = slice(h * HD, (h + 1) * HD)
            outs_t.append(mm(values_t[mine], probs))
            dqs_t.append(mm(keys_t[mine], grad_scores))
            dks.append(mm(grad_scores, query))
            dvs.append(nt(probs, grad_t))
        out_t = jnp.concatenate(outs_t, 0)
        column = lax.broadcasted_iota(jnp.int32, out_t.shape, 1)
        attn_t_ref[lanes] = jnp.where(column < valid_frames, out_t, 0.0).astype(BF)
        dq_ref[:, lanes] = (jnp.concatenate(dqs_t, 0) * scale).T.astype(BF)
        grad_key = ((dks[0] + dks[1]) * scale).astype(BF)
        grad_value = (dvs[0] + dvs[1]).astype(BF)
        dk_ref[:, lanes] = grad_key[:frames]
        dv_ref[:, lanes] = grad_value[:frames]
        dk_all[:, lanes] = grad_key[frames:]
        dv_all[:, lanes] = grad_value[frames:]

    for j in range(4):
        for k in range(4):
            place = meta[4 * j + k]
            rows = pl.ds(pl.multiple_of(BLK * jnp.maximum(place, 0), BLK), BLK)

            @pl.when(place >= 0)
            def _():
                back[j][k, 0] = dk_all[rows]
                back[j][k, 1] = dv_all[rows]

            @pl.when(place < 0)
            def _():
                back[j][k] = jnp.zeros(back[j].shape[1:], BF)


def attend(meta, query, own_keys, own_values, grad_attn, slots, entries, chunk, part, kept):
    frames, features = query.shape
    step = 2 * LANES
    first, offset = part[0] // step, (part[0] - chunk[0]) // step
    wide = pl.BlockSpec((frames, step), lambda i, m: (0, first + i))
    tall = pl.BlockSpec((step, frames), lambda i, m: (first + i, 0))
    slot = pl.BlockSpec((4, 2, BLK, step), lambda i, m: (0, 0, 0, offset + i))
    keys, blocks = frames + entries * BLK, entries * BLK
    rows = jax.ShapeDtypeStruct((frames, features), BF)
    return pl.pallas_call(
        attend_kernel,
        grid_spec=pltpu.PrefetchScalarGridSpec(
            num_scalar_prefetch=1,
            grid=(part[1] // step,),
            in_specs=[wide] * 3 + [tall] + [slot] * 4
            + [pl.BlockSpec(memory_space=pl.ANY)] * len(kept),
            out_specs=[tall] + [wide] * 3 + [slot] * 4,
            scratch_shapes=[pltpu.VMEM((keys, step), BF)] * 2
            + [pltpu.VMEM((blocks, step), BF)] * 2,
        ),
        out_shape=[jax.ShapeDtypeStruct((features, frames), BF)]
        + [rows] * 3
        + [jax.ShapeDtypeStruct((4, 2, BLK, chunk[1]), BF)] * 4,
        input_output_aliases={9 + i: i for i in range(len(kept))},
        compiler_params=pltpu.CompilerParams(vmem_limit_bytes=24 * MIB),
        cost_estimate=cost(part[1] // step * 4.6),
        name="attend",
    )(meta, query, own_keys, own_values, grad_attn, *slots, *kept)


def spread_slab(rows, ids):
    size, features = rows.shape
    note = jnp.pad(ids.astype(BF), (0, features - ids.shape[0]))[None]
    slab = jnp.concatenate([rows, note, jnp.zeros((15 - size, features), BF)], 0)
    return jnp.stack([slab] + [move(slab, 1, k) for k in range(1, 4)])


def gather_weight(slabs, size, place, before_z, before_core):
    z, core = lax.axis_index("z"), lax.axis_index("core")
    features = slabs[0].shape[-1]
    row = jnp.arange(16, dtype=jnp.int32)
    target = jnp.where(row < size, place.reshape(16, 1) * size + row, -1).reshape(1, 256)
    pick = (jnp.arange(16 * size, dtype=jnp.int32)[:, None] == target).astype(BF)
    rows = mm(pick, jnp.concatenate(slabs, 0).reshape(256, features)).astype(BF)
    rows = after(rows, *before_z)
    near = [shift(rows, "z", k) for k in (1, 3)]
    pieces = [rows, near[0], shift(after(rows, *near), "z", 2), near[1]]
    far = shift(after(jnp.stack(pieces), *before_core), "core", 1)
    from_z = (z - jnp.arange(4, dtype=jnp.int32)) % 4
    return pieces, far, jnp.concatenate([from_z * 2 + core, from_z * 2 + 1 - core])


def grad_attn_kernel(meta, grad_ref, *refs):
    pieces, out = [*refs[:4], *(refs[4].at[k] for k in range(4))], refs[5]
    size, frames = pieces[0].shape[0], grad_ref.shape[0]
    column = lax.broadcasted_iota(jnp.int32, (size, frames), 1)
    for i, piece in enumerate(pieces):
        part = jnp.where(column < meta[8] * BLK, nt(piece[...], grad_ref[...]), 0.0)
        out[pl.ds(pl.multiple_of(meta[i] * size, 32), size)] = part.astype(BF)


def grad_attn_rows(where, lengths, grad_rows, pieces, far):
    frames, features = grad_rows.shape
    return pl.pallas_call(
        grad_attn_kernel,
        in_specs=[pl.BlockSpec(memory_space=pltpu.SMEM)]
        + [pl.BlockSpec(memory_space=pltpu.VMEM)] * 6,
        out_specs=pl.BlockSpec(memory_space=pltpu.VMEM),
        out_shape=jax.ShapeDtypeStruct((features, frames), BF),
        compiler_params=pltpu.CompilerParams(vmem_limit_bytes=12 * MIB),
        cost_estimate=cost(4),
        name="grad_attn",
    )(jnp.concatenate([where, lengths]), grad_rows, *pieces, far)


def attended_kernel(where, attn_t_ref, *refs):
    pieces, out = [*refs[:4], *(refs[4].at[k] for k in range(4))], refs[5]
    size = pieces[0].shape[0]
    total = None
    for i, piece in enumerate(pieces):
        rows = attn_t_ref[pl.ds(pl.multiple_of(where[i] * size, 32), size)]
        part = mm(rows.T, piece[...])
        total = part if total is None else total + part
    out[...] = total.astype(BF)


def attended_rows(where, attn_t, pieces, far):
    features, frames = attn_t.shape
    wide = 2 * LANES
    size = features // 8
    return pl.pallas_call(
        attended_kernel,
        grid_spec=pltpu.PrefetchScalarGridSpec(
            num_scalar_prefetch=1,
            grid=(features // wide,),
            in_specs=[pl.BlockSpec((features, frames), lambda i, w: (0, 0))]
            + [pl.BlockSpec((size, wide), lambda i, w: (0, i))] * 4
            + [pl.BlockSpec((4, size, wide), lambda i, w: (0, 0, i))],
            out_specs=pl.BlockSpec((frames, wide), lambda i, w: (0, i)),
        ),
        out_shape=jax.ShapeDtypeStruct((frames, features), BF),
        compiler_params=pltpu.CompilerParams(vmem_limit_bytes=12 * MIB),
        cost_estimate=cost(4),
        name="attended",
    )(where, attn_t, *pieces, far)


def grad_weight_kernel(core, attn_t_ref, grad_ref, far_ref, near_ref):
    step = pl.program_id(0)
    part = mm(attn_t_ref[...], grad_ref[...])

    @pl.when(step < 4)
    def _():
        far_ref[0] = part.astype(BF)

    @pl.when(step >= 4)
    def _():
        near_ref[0] = part


def grad_weight_rows(attn_t, grad_rows, before_z, before_x):
    features, frames = attn_t.shape
    size = features // 8
    core, z = lax.axis_index("core"), lax.axis_index("z")
    far, near = pl.pallas_call(
        grad_weight_kernel,
        grid_spec=pltpu.PrefetchScalarGridSpec(
            num_scalar_prefetch=1,
            grid=(8,),
            in_specs=[
                pl.BlockSpec(
                    (size, frames),
                    lambda i, c: (jnp.where(i < 4, 2 * i + 1 - c[0], 2 * (i - 4) + c[0]), 0),
                ),
                pl.BlockSpec((frames, features), lambda i, c: (0, 0)),
            ],
            out_specs=[
                pl.BlockSpec((1, size, features), lambda i, c: (jnp.minimum(i, 3), 0, 0)),
                pl.BlockSpec((1, size, features), lambda i, c: (jnp.maximum(i - 4, 0), 0, 0)),
            ],
        ),
        out_shape=[
            jax.ShapeDtypeStruct((4, size, features), BF),
            jax.ShapeDtypeStruct((4, size, features), F32),
        ],
        compiler_params=pltpu.CompilerParams(vmem_limit_bytes=12 * MIB),
        cost_estimate=cost(5.5),
        name="grad_weight",
    )(core.reshape(1).astype(jnp.int32), attn_t, grad_rows)
    total = near + shift(far, "core", 1).astype(F32)
    total = after(total, *before_z).reshape(4 * size, features)
    for axis in ("z", "x", "y"):
        if axis == "x":
            total = after(total, *before_x)
        me = lax.axis_index(axis)
        rows = total.shape[0] // 4
        mine = lax.dynamic_slice_in_dim(total, me * rows, rows, 0)
        for k in range(1, 4):
            piece = lax.dynamic_slice_in_dim(total, (me + k) % 4 * rows, rows, 0)
            mine = mine + shift(piece.astype(BF), axis, k).astype(F32)
        total = mine
    return total


def body(queries, own_keys, own_values, lengths, history, cache_blocks, out_weight, grad_out):
    owned = cache_blocks.shape[0]
    x, y, core = (lax.axis_index(axis) for axis in ("x", "y", "core"))
    straight = core == 0
    first, second = jnp.where(straight, x, y), jnp.where(straight, y, x)
    steps = jnp.arange(4, dtype=jnp.int32)
    ids = history[0]
    owners = ids // owned
    owner_x, owner_y = owners // 4, owners % 4
    behind_first = (first - jnp.where(straight, owner_x, owner_y)) % 4
    behind_second = (second - jnp.where(straight, owner_y, owner_x)) % 4
    slot = behind_second * 4 + behind_first
    every = jnp.arange(16, dtype=jnp.int32)[:, None]
    rank = jnp.sum((slot[None, :] < every).astype(jnp.int32), axis=1)
    rank = jnp.where(jnp.any(slot[None, :] == every, axis=1), rank, -1)
    meta = jnp.concatenate([rank, lengths]).astype(jnp.int32)

    slab = spread_slab(out_weight, ids)
    note = slab[:, out_weight.shape[0], : ids.shape[0]].astype(jnp.int32)
    asked = jnp.stack([ids] + [note[4 - j] for j in range(1, 4)])
    along_first, along_second = (first - steps) % 4, (second - steps) % 4
    owner = jnp.where(straight, along_first * 4 + second, second * 4 + along_first)
    match = (asked // owned)[:, None, :] == owner[None, :, None]
    table = jnp.max(jnp.where(match, (asked % owned)[:, None, :], -1), axis=2)

    fetched, sends, arrived = [], [], []
    for number, (start, width) in enumerate(CHUNKS):
        part = lax.slice_in_dim(cache_blocks, start, start + width, axis=3)
        if number:
            part = after(part, slab)
        held = [part] + [move(part, 0, k) for k in range(1, 4)]
        arrived += held[1:]
        sent = select_rows(table, held)
        sends.append(sent[0])
        fetched.append([sent[0]] + [move(sent[j], 1, j) for j in range(1, 4)])

    place = jnp.where(
        straight,
        along_first[:, None] * 4 + along_second[None, :],
        along_second[None, :] * 4 + along_first[:, None],
    )
    slab = after(slab, arrived[0], arrived[2])
    slabs = [slab] + [move(slab, 0, k) for k in range(1, 4)]
    pieces, far, where = gather_weight(
        slabs, out_weight.shape[0], place, sends, fetched[0][1:]
    )
    grad_attn = grad_attn_rows(where, lengths, grad_out[0], pieces, far)

    own = (queries[0], own_keys[0], own_values[0])
    results, backs = (), []
    for chunk, parts, slots in zip(CHUNKS, PARTS, fetched):
        back = ()
        for number, part in enumerate(parts):
            if number == len(parts) - 1 and backs:
                grad_attn = after(grad_attn, *backs[-1][1:])
            out = attend(
                meta, *own, grad_attn, slots, ids.shape[0], chunk, part, (*results, *back)
            )
            results, back = out[:4], out[4:]
        backs.append([back[0]] + [move(back[j], 1, -j) for j in range(1, 4)])
    returned = []
    for back in backs:
        sums = fold_rows(table, back)
        returned.append([sums[0]] + [move(sums[k], 0, -k) for k in range(1, 4)])
    attn_t, *grads = results
    grad_cache = total_rows(returned)
    attended = attended_rows(where, attn_t, pieces, far)
    grad_weight = grad_weight_rows(attn_t, grad_out[0], (attended,), (returned[0][0],))
    return (attended[None], *(grad[None] for grad in grads), grad_cache, grad_weight)


def solution(mesh):
    axes = ("z", "core", "x", "y")
    fine = Mesh(mesh.devices.reshape(4, 2, 4, 4), axes)

    def split(rank):
        return P(axes, *([None] * (rank - 1)))

    return jax.shard_map(
        body,
        mesh=fine,
        in_specs=tuple(split(rank) for rank in (3, 3, 3, 1, 2, 4, 2, 3)),
        out_specs=tuple(split(rank) for rank in (3, 3, 3, 3, 4, 2)),
        check_vma=False,
    )
```

```python
import functools

import jax
import jax.numpy as jnp
from jax import lax
from jax.experimental import pallas as pl
from jax.experimental.pallas import tpu as pltpu
from jax.sharding import Mesh
from jax.sharding import PartitionSpec as P

HD = 64
BLK = 64
LANES = 128
LOG2E = 1.4426950408889634
BF = jnp.bfloat16
F32 = jnp.float32
MIB = 1024 * 1024
PARTS = ((0, 512), (512, 768))
STEP = 2 * LANES
PLANE = ("core", "x", "y")


def shift(array, axis, amount):
    n = lax.axis_size(axis)
    return lax.ppermute(array, axis, [(i, (i + amount) % n) for i in range(n)])


def move(array, leg, amount):
    pairs = []
    for core in range(2):
        for x in range(4):
            for y in range(4):
                along_x = (leg == 0) == (core == 0)
                to_x, to_y = ((x + amount) % 4, y) if along_x else (x, (y + amount) % 4)
                pairs.append((core * 16 + x * 4 + y, core * 16 + to_x * 4 + to_y))
    return lax.ppermute(array, PLANE, pairs)


def cost(us):
    return pl.CostEstimate(flops=int(us * 1.15e9), bytes_accessed=0, transcendentals=0)


def after(array, *earlier):
    return lax.optimization_barrier((array, earlier))[0]


def nt(a, b):
    return lax.dot_general(a, b, (((1,), (1,)), ((), ())), preferred_element_type=F32)


def mm(a, b):
    return lax.dot_general(a, b, (((1,), (0,)), ((), ())), preferred_element_type=F32)


def select_kernel(table, *refs):
    held, out = refs[:4], refs[4:]
    for j in range(4):
        for k in range(4):
            row = jnp.maximum(table[j * 4 + k], 0)
            out[j][k] = held[k][row]


def select_rows(table, held):
    _, kinds, rows, width = held[0].shape
    block_in = pl.BlockSpec((2, kinds, rows, STEP), lambda i, t: (0, 0, 0, i))
    block_out = pl.BlockSpec((4, kinds, rows, STEP), lambda i, t: (0, 0, 0, i))
    return pl.pallas_call(
        select_kernel,
        grid_spec=pltpu.PrefetchScalarGridSpec(
            num_scalar_prefetch=1,
            grid=(width // STEP,),
            in_specs=[block_in] * 4,
            out_specs=[block_out] * 4,
        ),
        out_shape=[jax.ShapeDtypeStruct((4, kinds, rows, width), BF)] * 4,
        compiler_params=pltpu.CompilerParams(vmem_limit_bytes=12 * MIB),
        cost_estimate=cost(3),
        name="select_rows",
    )(table.reshape(-1), *held)


def fold_kernel(table, *refs):
    out = refs[-4:]
    step = pl.program_id(0)
    for number, (start, width) in enumerate(PARTS):
        parts = refs[4 * number : 4 * number + 4]

        @pl.when((step >= start // STEP) & (step < (start + width) // STEP))
        def _():
            for k in range(4):
                for row in range(2):
                    total = None
                    for j in range(4):
                        keep = jnp.where(table[j * 4 + k] == row, 1.0, 0.0).astype(F32)
                        term = parts[j][k].astype(F32) * keep
                        total = term if total is None else total + term
                    out[k][row] = total.astype(BF)


def fold_rows(table, backs):
    _, kinds, rows, _ = backs[0][0].shape
    columns = sum(width for _, width in PARTS)
    blocks = []
    for start, width in PARTS:
        first, last = start // STEP, width // STEP - 1
        blocks += [
            pl.BlockSpec(
                (4, kinds, rows, STEP),
                lambda i, t, first=first, last=last: (0, 0, 0, jnp.clip(i - first, 0, last)),
            )
        ] * 4
    return pl.pallas_call(
        fold_kernel,
        grid_spec=pltpu.PrefetchScalarGridSpec(
            num_scalar_prefetch=1,
            grid=(columns // STEP,),
            in_specs=blocks,
            out_specs=[pl.BlockSpec((2, kinds, rows, STEP), lambda i, t: (0, 0, 0, i))] * 4,
        ),
        out_shape=[jax.ShapeDtypeStruct((2, kinds, rows, columns), BF)] * 4,
        compiler_params=pltpu.CompilerParams(vmem_limit_bytes=16 * MIB),
        cost_estimate=cost(4),
        name="fold_rows",
    )(table.reshape(-1), *backs[0], *backs[1])


def total_kernel(*refs):
    total = refs[0][...].astype(F32)
    for part in refs[1:-1]:
        total = total + part[...].astype(F32)
    refs[-1][...] = total


def total_rows(parts):
    owned, kinds, rows, width = parts[0].shape
    block = pl.BlockSpec((owned, kinds, rows, STEP), lambda i: (0, 0, 0, i))
    return pl.pallas_call(
        total_kernel,
        grid=(width // STEP,),
        in_specs=[block] * 4,
        out_specs=block,
        out_shape=jax.ShapeDtypeStruct((owned, kinds, rows, width), F32),
        compiler_params=pltpu.CompilerParams(vmem_limit_bytes=12 * MIB),
        cost_estimate=cost(4),
        name="total_rows",
    )(*parts)


def head_front(keys, values, query, grad_t, head):
    lane = lax.broadcasted_iota(jnp.int32, query.shape, 1) // HD
    feature = lax.broadcasted_iota(jnp.int32, grad_t.shape, 0) // HD
    query = jnp.where(lane == head, query, jnp.zeros_like(query))
    grad_t = jnp.where(feature == head, grad_t, jnp.zeros_like(grad_t))
    return query, grad_t, nt(keys, query), mm(values, grad_t)


def head_softmax(scores, grad_probs, valid_frames):
    frames = scores.shape[1]
    key_row = lax.broadcasted_iota(jnp.int32, (frames, frames), 0)
    own = jnp.where(key_row < valid_frames, scores[:frames], -1e30)
    scores = jnp.concatenate([own, scores[frames:]], 0)
    top = jnp.max(scores, axis=0, keepdims=True)
    expo = jnp.exp2((scores - top) * (HD**-0.5 * LOG2E))
    probs = expo * (1.0 / jnp.sum(expo, axis=0, keepdims=True))
    row_dots = jnp.sum(probs * grad_probs, axis=0, keepdims=True)
    return probs.astype(BF), (probs * (grad_probs - row_dots)).astype(BF)


def attend_kernel(meta, q_ref, ko_ref, vo_ref, g_ref, *refs):
    slots = refs[:4]
    attn_t_ref, dq_ref, dk_ref, dv_ref = refs[-12:-8]
    back, (k_all, v_all, dk_all, dv_all) = refs[-8:-4], refs[-4:]
    frames, width = q_ref.shape
    scale = HD**-0.5
    valid_frames = meta[16] * BLK
    k_all[:frames] = ko_ref[...]
    v_all[:frames] = vo_ref[...]

    def rows_of(place):
        return pl.ds(pl.multiple_of(frames + BLK * jnp.maximum(place, 0), BLK), BLK)

    for j in range(4):
        for k in range(4):
            place = meta[4 * j + k]

            @pl.when(place >= 0)
            def _():
                k_all[rows_of(place)] = slots[j][k, 0]
                v_all[rows_of(place)] = slots[j][k, 1]

    for pair in range(width // LANES):
        lanes = slice(pair * LANES, (pair + 1) * LANES)
        keys, values = k_all[:, lanes], v_all[:, lanes]
        keys_t, values_t = keys.T, values.T
        fronts = [head_front(keys, values, q_ref[:, lanes], g_ref[lanes], h) for h in range(2)]
        outs_t, dqs_t, dks, dvs = [], [], [], []
        for h, (query, grad_t, scores, grad_probs) in enumerate(fronts):
            probs, grad_scores = head_softmax(scores, grad_probs, valid_frames)
            mine = slice(h * HD, (h + 1) * HD)
            outs_t.append(mm(values_t[mine], probs))
            dqs_t.append(mm(keys_t[mine], grad_scores))
            dks.append(mm(grad_scores, query))
            dvs.append(nt(probs, grad_t))
        out_t = jnp.concatenate(outs_t, 0)
        column = lax.broadcasted_iota(jnp.int32, out_t.shape, 1)
        attn_t_ref[lanes] = jnp.where(column < valid_frames, out_t, 0.0).astype(BF)
        dq_ref[:, lanes] = (jnp.concatenate(dqs_t, 0) * scale).T.astype(BF)
        grad_key = ((dks[0] + dks[1]) * scale).astype(BF)
        grad_value = (dvs[0] + dvs[1]).astype(BF)
        dk_ref[:, lanes] = grad_key[:frames]
        dv_ref[:, lanes] = grad_value[:frames]
        dk_all[:, lanes] = grad_key[frames:]
        dv_all[:, lanes] = grad_value[frames:]

    for j in range(4):
        for k in range(4):
            place = meta[4 * j + k]
            rows = pl.ds(pl.multiple_of(BLK * jnp.maximum(place, 0), BLK), BLK)

            @pl.when(place >= 0)
            def _():
                back[j][k, 0] = dk_all[rows]
                back[j][k, 1] = dv_all[rows]

            @pl.when(place < 0)
            def _():
                back[j][k] = jnp.zeros(back[j].shape[1:], BF)


def attend(meta, query, own_keys, own_values, grad_attn, slots, entries, part, kept):
    frames, features = query.shape
    first = part[0] // STEP
    wide = pl.BlockSpec((frames, STEP), lambda i, m: (0, first + i))
    tall = pl.BlockSpec((STEP, frames), lambda i, m: (first + i, 0))
    slot = pl.BlockSpec((4, 2, BLK, STEP), lambda i, m: (0, 0, 0, first + i))
    back = pl.BlockSpec((4, 2, BLK, STEP), lambda i, m: (0, 0, 0, i))
    keys, blocks = frames + entries * BLK, entries * BLK
    rows = jax.ShapeDtypeStruct((frames, features), BF)
    return pl.pallas_call(
        attend_kernel,
        grid_spec=pltpu.PrefetchScalarGridSpec(
            num_scalar_prefetch=1,
            grid=(part[1] // STEP,),
            in_specs=[wide] * 3 + [tall] + [slot] * 4
            + [pl.BlockSpec(memory_space=pl.ANY)] * len(kept),
            out_specs=[tall] + [wide] * 3 + [back] * 4,
            scratch_shapes=[pltpu.VMEM((keys, STEP), BF)] * 2
            + [pltpu.VMEM((blocks, STEP), BF)] * 2,
        ),
        out_shape=[jax.ShapeDtypeStruct((features, frames), BF)]
        + [rows] * 3
        + [jax.ShapeDtypeStruct((4, 2, BLK, part[1]), BF)] * 4,
        input_output_aliases={9 + i: i for i in range(len(kept))},
        compiler_params=pltpu.CompilerParams(vmem_limit_bytes=24 * MIB),
        cost_estimate=cost(part[1] // STEP * 4.6),
        name="attend",
    )(meta, query, own_keys, own_values, grad_attn, *slots, *kept)


def spread_slab(rows, ids):
    size, features = rows.shape
    note = jnp.pad(ids.astype(BF), (0, features - ids.shape[0]))[None]
    slab = jnp.concatenate([rows, note, jnp.zeros((15 - size, features), BF)], 0)
    return jnp.stack([slab] + [move(slab, 1, k) for k in range(1, 4)])


def gather_weight(slabs, size, place, before_z, before_core):
    z, core = lax.axis_index("z"), lax.axis_index("core")
    features = slabs[0].shape[-1]
    row = jnp.arange(16, dtype=jnp.int32)
    target = jnp.where(row < size, place.reshape(16, 1) * size + row, -1).reshape(1, 256)
    pick = (jnp.arange(16 * size, dtype=jnp.int32)[:, None] == target).astype(BF)
    rows = mm(pick, jnp.concatenate(slabs, 0).reshape(256, features)).astype(BF)
    rows = after(rows, *before_z)
    pieces = [rows] + [shift(rows, "z", k) for k in range(1, 4)]
    far = [shift(piece, "core", 1) for piece in pieces]
    from_z = (z - jnp.arange(4, dtype=jnp.int32)) % 4
    return pieces, far, jnp.concatenate([from_z * 2 + core, from_z * 2 + 1 - core])


def grad_attn_kernel(meta, grad_ref, *refs):
    pieces, out = refs[:8], refs[8]
    size, frames = pieces[0].shape[0], grad_ref.shape[0]
    column = lax.broadcasted_iota(jnp.int32, (size, frames), 1)
    for i, piece in enumerate(pieces):
        part = jnp.where(column < meta[8] * BLK, nt(piece[...], grad_ref[...]), 0.0)
        out[pl.ds(pl.multiple_of(meta[i] * size, 32), size)] = part.astype(BF)


def grad_attn_rows(where, lengths, grad_rows, pieces, far):
    frames, features = grad_rows.shape
    return pl.pallas_call(
        grad_attn_kernel,
        in_specs=[pl.BlockSpec(memory_space=pltpu.SMEM)]
        + [pl.BlockSpec(memory_space=pltpu.VMEM)] * 9,
        out_specs=pl.BlockSpec(memory_space=pltpu.VMEM),
        out_shape=jax.ShapeDtypeStruct((features, frames), BF),
        compiler_params=pltpu.CompilerParams(vmem_limit_bytes=12 * MIB),
        cost_estimate=cost(4),
        name="grad_attn",
    )(jnp.concatenate([where, lengths]), grad_rows, *pieces, *far)


def attended_kernel(where, attn_t_ref, *refs):
    pieces, out = refs[:8], refs[8]
    size = pieces[0].shape[0]
    total = None
    for i, piece in enumerate(pieces):
        rows = attn_t_ref[pl.ds(pl.multiple_of(where[i] * size, 32), size)]
        part = mm(rows.T, piece[...])
        total = part if total is None else total + part
    out[...] = total.astype(BF)


def attended_rows(where, attn_t, pieces, far):
    features, frames = attn_t.shape
    wide = 2 * LANES
    size = features // 8
    return pl.pallas_call(
        attended_kernel,
        grid_spec=pltpu.PrefetchScalarGridSpec(
            num_scalar_prefetch=1,
            grid=(features // wide,),
            in_specs=[pl.BlockSpec((features, frames), lambda i, w: (0, 0))]
            + [pl.BlockSpec((size, wide), lambda i, w: (0, i))] * 8,
            out_specs=pl.BlockSpec((frames, wide), lambda i, w: (0, i)),
        ),
        out_shape=jax.ShapeDtypeStruct((frames, features), BF),
        compiler_params=pltpu.CompilerParams(vmem_limit_bytes=58 * MIB),
        cost_estimate=cost(0.1),
        name="attended",
    )(where, attn_t, *pieces, *far)


def grad_weight_kernel(core, attn_t_ref, grad_ref, far_ref, near_ref):
    step = pl.program_id(0)
    part = mm(attn_t_ref[...], grad_ref[...])

    @pl.when(step < 4)
    def _():
        far_ref[0] = part.astype(BF)

    @pl.when(step >= 4)
    def _():
        near_ref[0] = part


def grad_weight_rows(attn_t, grad_rows):
    features, frames = attn_t.shape
    size = features // 8
    core, z = lax.axis_index("core"), lax.axis_index("z")
    far, near = pl.pallas_call(
        grad_weight_kernel,
        grid_spec=pltpu.PrefetchScalarGridSpec(
            num_scalar_prefetch=1,
            grid=(8,),
            in_specs=[
                pl.BlockSpec(
                    (size, frames),
                    lambda i, c: (jnp.where(i < 4, 2 * i + 1 - c[0], 2 * (i - 4) + c[0]), 0),
                ),
                pl.BlockSpec((frames, features), lambda i, c: (0, 0)),
            ],
            out_specs=[
                pl.BlockSpec((1, size, features), lambda i, c: (jnp.minimum(i, 3), 0, 0)),
                pl.BlockSpec((1, size, features), lambda i, c: (jnp.maximum(i - 4, 0), 0, 0)),
            ],
        ),
        out_shape=[
            jax.ShapeDtypeStruct((4, size, features), BF),
            jax.ShapeDtypeStruct((4, size, features), F32),
        ],
        compiler_params=pltpu.CompilerParams(vmem_limit_bytes=12 * MIB),
        cost_estimate=cost(0.1),
        name="grad_weight",
    )(core.reshape(1).astype(jnp.int32), attn_t, grad_rows)
    total = near + shift(far, "core", 1).astype(F32)
    return total.reshape(4 * size, features)


def begin_sum(total, axis):
    me = lax.axis_index(axis)
    rows = total.shape[0] // 4
    pieces = [lax.dynamic_slice_in_dim(total, (me + k) % 4 * rows, rows, 0) for k in range(4)]
    return pieces[0], pieces[2].astype(BF), [shift(pieces[k].astype(BF), axis, k) for k in (1, 3)]


def end_sum(own, opposite, near, axis):
    for piece in (*near, shift(opposite, axis, 2)):
        own = own + piece.astype(F32)
    return own


def body(queries, own_keys, own_values, lengths, history, cache_blocks, out_weight, grad_out):
    owned = cache_blocks.shape[0]
    x, y, core = (lax.axis_index(axis) for axis in ("x", "y", "core"))
    straight = core == 0
    first, second = jnp.where(straight, x, y), jnp.where(straight, y, x)
    steps = jnp.arange(4, dtype=jnp.int32)
    ids = history[0]
    owners = ids // owned
    owner_x, owner_y = owners // 4, owners % 4
    behind_first = (first - jnp.where(straight, owner_x, owner_y)) % 4
    behind_second = (second - jnp.where(straight, owner_y, owner_x)) % 4
    slot = behind_second * 4 + behind_first
    every = jnp.arange(16, dtype=jnp.int32)[:, None]
    rank = jnp.sum((slot[None, :] < every).astype(jnp.int32), axis=1)
    rank = jnp.where(jnp.any(slot[None, :] == every, axis=1), rank, -1)
    meta = jnp.concatenate([rank, lengths]).astype(jnp.int32)

    slab = spread_slab(out_weight, ids)
    note = slab[:, out_weight.shape[0], : ids.shape[0]].astype(jnp.int32)
    asked = jnp.stack([ids] + [note[4 - j] for j in range(1, 4)])
    along_first, along_second = (first - steps) % 4, (second - steps) % 4
    owner = jnp.where(straight, along_first * 4 + second, second * 4 + along_first)
    match = (asked // owned)[:, None, :] == owner[None, :, None]
    table = jnp.max(jnp.where(match, (asked % owned)[:, None, :], -1), axis=2)

    held = [cache_blocks] + [move(cache_blocks, 0, k) for k in range(1, 4)]
    sent = select_rows(table, held)
    slots = [sent[0]] + [move(sent[j], 1, j) for j in range(1, 4)]

    place = jnp.where(
        straight,
        along_first[:, None] * 4 + along_second[None, :],
        along_second[None, :] * 4 + along_first[:, None],
    )
    slab = after(slab, held[1])
    slabs = [slab] + [move(slab, 0, k) for k in range(1, 4)]
    pieces, far, where = gather_weight(
        slabs, out_weight.shape[0], place, sent[:1], ()
    )
    grad_attn = grad_attn_rows(where, lengths, after(grad_out[0], *slots[1:]), pieces, far)

    own = (queries[0], own_keys[0], own_values[0])
    results, backs = (), []
    for part in PARTS:
        out = attend(meta, *own, grad_attn, slots, ids.shape[0], part, results)
        results, back = out[:4], out[4:]
        backs.append([back[0]] + [move(back[j], 1, -j) for j in range(1, 4)])
    attn_t, *grads = results
    total = grad_weight_rows(after(attn_t, *backs[0][1:]), grad_out[0])
    own, opposite, near = begin_sum(total, "z")
    sums = fold_rows(table, backs)
    total = end_sum(after(own, sums[0]), opposite, near, "z")
    total = end_sum(*begin_sum(total, "x"), "x")
    attended = attended_rows(where, after(attn_t, total), pieces, far)
    grad_weight = end_sum(*begin_sum(total, "y"), "y")
    mine = after(sums[0], attended)
    grad_cache = total_rows([mine] + [move(sums[k], 0, -k) for k in range(1, 4)])
    return (attended[None], *(grad[None] for grad in grads), grad_cache, grad_weight)


def solution(mesh):
    axes = ("z", "core", "x", "y")
    fine = Mesh(mesh.devices.reshape(4, 2, 4, 4), axes)

    def split(rank):
        return P(axes, *([None] * (rank - 1)))

    return jax.shard_map(
        body,
        mesh=fine,
        in_specs=tuple(split(rank) for rank in (3, 3, 3, 1, 2, 4, 2, 3)),
        out_specs=tuple(split(rank) for rank in (3, 3, 3, 3, 4, 2)),
        check_vma=False,
    )
```

```python
import functools

import jax
import jax.numpy as jnp
from jax import lax
from jax.experimental import pallas as pl
from jax.experimental.pallas import tpu as pltpu
from jax.sharding import Mesh
from jax.sharding import PartitionSpec as P

HD = 64
BLK = 64
LANES = 128
LOG2E = 1.4426950408889634
BF = jnp.bfloat16
F32 = jnp.float32
MIB = 1024 * 1024
PARTS = ((0, 512), (512, 768))
STEP = 2 * LANES
PLANE = ("core", "x", "y")


def shift(array, axis, amount):
    n = lax.axis_size(axis)
    return lax.ppermute(array, axis, [(i, (i + amount) % n) for i in range(n)])


def move(array, leg, amount):
    pairs = []
    for core in range(2):
        for x in range(4):
            for y in range(4):
                along_x = (leg == 0) == (core == 0)
                to_x, to_y = ((x + amount) % 4, y) if along_x else (x, (y + amount) % 4)
                pairs.append((core * 16 + x * 4 + y, core * 16 + to_x * 4 + to_y))
    return lax.ppermute(array, PLANE, pairs)


def cost(us):
    return pl.CostEstimate(flops=int(us * 1.15e9), bytes_accessed=0, transcendentals=0)


def after(array, *earlier):
    return lax.optimization_barrier((array, earlier))[0]


def nt(a, b):
    return lax.dot_general(a, b, (((1,), (1,)), ((), ())), preferred_element_type=F32)


def mm(a, b):
    return lax.dot_general(a, b, (((1,), (0,)), ((), ())), preferred_element_type=F32)


def select_kernel(table, *refs):
    held, out = refs[:4], refs[4:]
    for j in range(4):
        for k in range(4):
            row = jnp.maximum(table[j * 4 + k], 0)
            out[j][k] = held[k][row]


def select_rows(table, held):
    _, kinds, rows, width = held[0].shape
    block_in = pl.BlockSpec((2, kinds, rows, STEP), lambda i, t: (0, 0, 0, i))
    block_out = pl.BlockSpec((4, kinds, rows, STEP), lambda i, t: (0, 0, 0, i))
    return pl.pallas_call(
        select_kernel,
        grid_spec=pltpu.PrefetchScalarGridSpec(
            num_scalar_prefetch=1,
            grid=(width // STEP,),
            in_specs=[block_in] * 4,
            out_specs=[block_out] * 4,
        ),
        out_shape=[jax.ShapeDtypeStruct((4, kinds, rows, width), BF)] * 4,
        compiler_params=pltpu.CompilerParams(vmem_limit_bytes=12 * MIB),
        cost_estimate=cost(3),
        name="select_rows",
    )(table.reshape(-1), *held)


def fold_kernel(table, *refs):
    out = refs[-4:]
    step = pl.program_id(0)
    for number, (start, width) in enumerate(PARTS):
        parts = refs[4 * number : 4 * number + 4]

        @pl.when((step >= start // STEP) & (step < (start + width) // STEP))
        def _():
            for k in range(4):
                for row in range(2):
                    total = None
                    for j in range(4):
                        keep = jnp.where(table[j * 4 + k] == row, 1.0, 0.0).astype(F32)
                        term = parts[j][k].astype(F32) * keep
                        total = term if total is None else total + term
                    out[k][row] = total.astype(BF)


def fold_rows(table, backs):
    _, kinds, rows, _ = backs[0][0].shape
    columns = sum(width for _, width in PARTS)
    blocks = []
    for start, width in PARTS:
        first, last = start // STEP, width // STEP - 1
        blocks += [
            pl.BlockSpec(
                (4, kinds, rows, STEP),
                lambda i, t, first=first, last=last: (0, 0, 0, jnp.clip(i - first, 0, last)),
            )
        ] * 4
    return pl.pallas_call(
        fold_kernel,
        grid_spec=pltpu.PrefetchScalarGridSpec(
            num_scalar_prefetch=1,
            grid=(columns // STEP,),
            in_specs=blocks,
            out_specs=[pl.BlockSpec((2, kinds, rows, STEP), lambda i, t: (0, 0, 0, i))] * 4,
        ),
        out_shape=[jax.ShapeDtypeStruct((2, kinds, rows, columns), BF)] * 4,
        compiler_params=pltpu.CompilerParams(vmem_limit_bytes=58 * MIB),
        cost_estimate=cost(4),
        name="fold_rows",
    )(table.reshape(-1), *backs[0], *backs[1])


def total_kernel(*refs):
    total = refs[0][...].astype(F32)
    for part in refs[1:-1]:
        total = total + part[...].astype(F32)
    refs[-1][...] = total


def total_rows(parts):
    owned, kinds, rows, width = parts[0].shape
    block = pl.BlockSpec((owned, kinds, rows, STEP), lambda i: (0, 0, 0, i))
    return pl.pallas_call(
        total_kernel,
        grid=(width // STEP,),
        in_specs=[block] * 4,
        out_specs=block,
        out_shape=jax.ShapeDtypeStruct((owned, kinds, rows, width), F32),
        compiler_params=pltpu.CompilerParams(vmem_limit_bytes=12 * MIB),
        cost_estimate=cost(4),
        name="total_rows",
    )(*parts)


def head_front(keys, values, query, grad_t, head):
    lane = lax.broadcasted_iota(jnp.int32, query.shape, 1) // HD
    feature = lax.broadcasted_iota(jnp.int32, grad_t.shape, 0) // HD
    query = jnp.where(lane == head, query, jnp.zeros_like(query))
    grad_t = jnp.where(feature == head, grad_t, jnp.zeros_like(grad_t))
    return query, grad_t, nt(keys, query), mm(values, grad_t)


def head_softmax(scores, grad_probs, valid_frames):
    frames = scores.shape[1]
    key_row = lax.broadcasted_iota(jnp.int32, (frames, frames), 0)
    own = jnp.where(key_row < valid_frames, scores[:frames], -1e30)
    scores = jnp.concatenate([own, scores[frames:]], 0)
    top = jnp.max(scores, axis=0, keepdims=True)
    expo = jnp.exp2((scores - top) * (HD**-0.5 * LOG2E))
    probs = expo * (1.0 / jnp.sum(expo, axis=0, keepdims=True))
    row_dots = jnp.sum(probs * grad_probs, axis=0, keepdims=True)
    return probs.astype(BF), (probs * (grad_probs - row_dots)).astype(BF)


def attend_kernel(meta, q_ref, ko_ref, vo_ref, g_ref, *refs):
    slots = refs[:4]
    attn_t_ref, dq_ref, dk_ref, dv_ref = refs[-12:-8]
    back, (k_all, v_all, dk_all, dv_all) = refs[-8:-4], refs[-4:]
    frames, width = q_ref.shape
    scale = HD**-0.5
    valid_frames = meta[16] * BLK
    k_all[:frames] = ko_ref[...]
    v_all[:frames] = vo_ref[...]

    def rows_of(place):
        return pl.ds(pl.multiple_of(frames + BLK * jnp.maximum(place, 0), BLK), BLK)

    for j in range(4):
        for k in range(4):
            place = meta[4 * j + k]

            @pl.when(place >= 0)
            def _():
                k_all[rows_of(place)] = slots[j][k, 0]
                v_all[rows_of(place)] = slots[j][k, 1]

    for pair in range(width // LANES):
        lanes = slice(pair * LANES, (pair + 1) * LANES)
        keys, values = k_all[:, lanes], v_all[:, lanes]
        keys_t, values_t = keys.T, values.T
        fronts = [head_front(keys, values, q_ref[:, lanes], g_ref[lanes], h) for h in range(2)]
        outs_t, dqs_t, dks, dvs = [], [], [], []
        for h, (query, grad_t, scores, grad_probs) in enumerate(fronts):
            probs, grad_scores = head_softmax(scores, grad_probs, valid_frames)
            mine = slice(h * HD, (h + 1) * HD)
            outs_t.append(mm(values_t[mine], probs))
            dqs_t.append(mm(keys_t[mine], grad_scores))
            dks.append(mm(grad_scores, query))
            dvs.append(nt(probs, grad_t))
        out_t = jnp.concatenate(outs_t, 0)
        column = lax.broadcasted_iota(jnp.int32, out_t.shape, 1)
        attn_t_ref[lanes] = jnp.where(column < valid_frames, out_t, 0.0).astype(BF)
        dq_ref[:, lanes] = (jnp.concatenate(dqs_t, 0) * scale).T.astype(BF)
        grad_key = ((dks[0] + dks[1]) * scale).astype(BF)
        grad_value = (dvs[0] + dvs[1]).astype(BF)
        dk_ref[:, lanes] = grad_key[:frames]
        dv_ref[:, lanes] = grad_value[:frames]
        dk_all[:, lanes] = grad_key[frames:]
        dv_all[:, lanes] = grad_value[frames:]

    for j in range(4):
        for k in range(4):
            place = meta[4 * j + k]
            rows = pl.ds(pl.multiple_of(BLK * jnp.maximum(place, 0), BLK), BLK)

            @pl.when(place >= 0)
            def _():
                back[j][k, 0] = dk_all[rows]
                back[j][k, 1] = dv_all[rows]

            @pl.when(place < 0)
            def _():
                back[j][k] = jnp.zeros(back[j].shape[1:], BF)


def attend(meta, query, own_keys, own_values, grad_attn, slots, entries, part, kept):
    frames, features = query.shape
    first = part[0] // STEP
    wide = pl.BlockSpec((frames, STEP), lambda i, m: (0, first + i))
    tall = pl.BlockSpec((STEP, frames), lambda i, m: (first + i, 0))
    slot = pl.BlockSpec((4, 2, BLK, STEP), lambda i, m: (0, 0, 0, first + i))
    back = pl.BlockSpec((4, 2, BLK, STEP), lambda i, m: (0, 0, 0, i))
    keys, blocks = frames + entries * BLK, entries * BLK
    rows = jax.ShapeDtypeStruct((frames, features), BF)
    return pl.pallas_call(
        attend_kernel,
        grid_spec=pltpu.PrefetchScalarGridSpec(
            num_scalar_prefetch=1,
            grid=(part[1] // STEP,),
            in_specs=[wide] * 3 + [tall] + [slot] * 4
            + [pl.BlockSpec(memory_space=pl.ANY)] * len(kept),
            out_specs=[tall] + [wide] * 3 + [back] * 4,
            scratch_shapes=[pltpu.VMEM((keys, STEP), BF)] * 2
            + [pltpu.VMEM((blocks, STEP), BF)] * 2,
        ),
        out_shape=[jax.ShapeDtypeStruct((features, frames), BF)]
        + [rows] * 3
        + [jax.ShapeDtypeStruct((4, 2, BLK, part[1]), BF)] * 4,
        input_output_aliases={9 + i: i for i in range(len(kept))},
        compiler_params=pltpu.CompilerParams(vmem_limit_bytes=58 * MIB),
        cost_estimate=cost(part[1] // STEP * 4.6),
        name="attend",
    )(meta, query, own_keys, own_values, grad_attn, *slots, *kept)


def spread_slab(rows, ids):
    size, features = rows.shape
    note = jnp.pad(ids.astype(BF), (0, features - ids.shape[0]))[None]
    slab = jnp.concatenate([rows, note, jnp.zeros((15 - size, features), BF)], 0)
    return jnp.stack([slab] + [move(slab, 1, k) for k in range(1, 4)])


def gather_weight(slabs, size, place, before_z, before_core):
    z, core = lax.axis_index("z"), lax.axis_index("core")
    features = slabs[0].shape[-1]
    row = jnp.arange(16, dtype=jnp.int32)
    target = jnp.where(row < size, place.reshape(16, 1) * size + row, -1).reshape(1, 256)
    pick = (jnp.arange(16 * size, dtype=jnp.int32)[:, None] == target).astype(BF)
    rows = mm(pick, jnp.concatenate(slabs, 0).reshape(256, features)).astype(BF)
    rows = after(rows, *before_z)
    pieces = [rows] + [shift(rows, "z", k) for k in range(1, 4)]
    far = [shift(piece, "core", 1) for piece in pieces]
    from_z = (z - jnp.arange(4, dtype=jnp.int32)) % 4
    return pieces, far, jnp.concatenate([from_z * 2 + core, from_z * 2 + 1 - core])


def grad_attn_kernel(meta, grad_ref, *refs):
    pieces, out = refs[:8], refs[8]
    size, frames = pieces[0].shape[0], grad_ref.shape[0]
    column = lax.broadcasted_iota(jnp.int32, (size, frames), 1)
    for i, piece in enumerate(pieces):
        part = jnp.where(column < meta[8] * BLK, nt(piece[...], grad_ref[...]), 0.0)
        out[pl.ds(pl.multiple_of(meta[i] * size, 32), size)] = part.astype(BF)


def grad_attn_rows(where, lengths, grad_rows, pieces, far):
    frames, features = grad_rows.shape
    return pl.pallas_call(
        grad_attn_kernel,
        in_specs=[pl.BlockSpec(memory_space=pltpu.SMEM)]
        + [pl.BlockSpec(memory_space=pltpu.VMEM)] * 9,
        out_specs=pl.BlockSpec(memory_space=pltpu.VMEM),
        out_shape=jax.ShapeDtypeStruct((features, frames), BF),
        compiler_params=pltpu.CompilerParams(vmem_limit_bytes=12 * MIB),
        cost_estimate=cost(4),
        name="grad_attn",
    )(jnp.concatenate([where, lengths]), grad_rows, *pieces, *far)


def attended_kernel(where, attn_t_ref, *refs):
    pieces, out = refs[:8], refs[8]
    size = pieces[0].shape[0]
    total = None
    for i, piece in enumerate(pieces):
        rows = attn_t_ref[pl.ds(pl.multiple_of(where[i] * size, 32), size)]
        part = mm(rows.T, piece[...])
        total = part if total is None else total + part
    out[...] = total.astype(BF)


def attended_rows(where, attn_t, pieces, far):
    features, frames = attn_t.shape
    wide = 2 * LANES
    size = features // 8
    return pl.pallas_call(
        attended_kernel,
        grid_spec=pltpu.PrefetchScalarGridSpec(
            num_scalar_prefetch=1,
            grid=(features // wide,),
            in_specs=[pl.BlockSpec((features, frames), lambda i, w: (0, 0))]
            + [pl.BlockSpec((size, wide), lambda i, w: (0, i))] * 8,
            out_specs=pl.BlockSpec((frames, wide), lambda i, w: (0, i)),
        ),
        out_shape=jax.ShapeDtypeStruct((frames, features), BF),
        compiler_params=pltpu.CompilerParams(vmem_limit_bytes=58 * MIB),
        cost_estimate=cost(0.1),
        name="attended",
    )(where, attn_t, *pieces, *far)


def grad_weight_kernel(core, attn_t_ref, grad_ref, out_ref):
    out_ref[0] = mm(attn_t_ref[...], grad_ref[...]).astype(out_ref.dtype)


def grad_weight_half(core, attn_t, grad_rows, dtype):
    features, frames = attn_t.shape
    size = features // 8
    return pl.pallas_call(
        grad_weight_kernel,
        grid_spec=pltpu.PrefetchScalarGridSpec(
            num_scalar_prefetch=1,
            grid=(4,),
            in_specs=[
                pl.BlockSpec((size, frames), lambda i, c: (2 * i + c[0], 0)),
                pl.BlockSpec((frames, features), lambda i, c: (0, 0)),
            ],
            out_specs=pl.BlockSpec((1, size, features), lambda i, c: (i, 0, 0)),
        ),
        out_shape=jax.ShapeDtypeStruct((4, size, features), dtype),
        compiler_params=pltpu.CompilerParams(vmem_limit_bytes=12 * MIB),
        cost_estimate=cost(0.1),
        name="grad_weight",
    )(core.reshape(1).astype(jnp.int32), attn_t, grad_rows)


def grad_weight_rows(attn_t, grad_rows):
    core = lax.axis_index("core")
    far = grad_weight_half(1 - core, attn_t, grad_rows, BF)
    near = grad_weight_half(core, attn_t, grad_rows, F32)
    total = near + shift(far, "core", 1).astype(F32)
    return total.reshape(-1, grad_rows.shape[1])


def begin_sum(total, axis):
    me = lax.axis_index(axis)
    rows = total.shape[0] // 4
    pieces = [lax.dynamic_slice_in_dim(total, (me + k) % 4 * rows, rows, 0) for k in range(4)]
    return pieces[0], pieces[2].astype(BF), [shift(pieces[k].astype(BF), axis, k) for k in (1, 3)]


def end_sum(own, opposite, near, axis):
    for piece in (*near, shift(opposite, axis, 2)):
        own = own + piece.astype(F32)
    return own


def body(queries, own_keys, own_values, lengths, history, cache_blocks, out_weight, grad_out):
    owned = cache_blocks.shape[0]
    x, y, core = (lax.axis_index(axis) for axis in ("x", "y", "core"))
    straight = core == 0
    first, second = jnp.where(straight, x, y), jnp.where(straight, y, x)
    steps = jnp.arange(4, dtype=jnp.int32)
    ids = history[0]
    owners = ids // owned
    owner_x, owner_y = owners // 4, owners % 4
    behind_first = (first - jnp.where(straight, owner_x, owner_y)) % 4
    behind_second = (second - jnp.where(straight, owner_y, owner_x)) % 4
    slot = behind_second * 4 + behind_first
    every = jnp.arange(16, dtype=jnp.int32)[:, None]
    rank = jnp.sum((slot[None, :] < every).astype(jnp.int32), axis=1)
    rank = jnp.where(jnp.any(slot[None, :] == every, axis=1), rank, -1)
    meta = jnp.concatenate([rank, lengths]).astype(jnp.int32)

    slab = spread_slab(out_weight, ids)
    note = slab[:, out_weight.shape[0], : ids.shape[0]].astype(jnp.int32)
    asked = jnp.stack([ids] + [note[4 - j] for j in range(1, 4)])
    along_first, along_second = (first - steps) % 4, (second - steps) % 4
    owner = jnp.where(straight, along_first * 4 + second, second * 4 + along_first)
    match = (asked // owned)[:, None, :] == owner[None, :, None]
    table = jnp.max(jnp.where(match, (asked % owned)[:, None, :], -1), axis=2)

    held = [cache_blocks] + [move(cache_blocks, 0, k) for k in range(1, 4)]
    sent = select_rows(table, held)
    slots = [sent[0]] + [move(sent[j], 1, j) for j in range(1, 4)]

    place = jnp.where(
        straight,
        along_first[:, None] * 4 + along_second[None, :],
        along_second[None, :] * 4 + along_first[:, None],
    )
    slab = after(slab, held[1])
    slabs = [slab] + [move(slab, 0, k) for k in range(1, 4)]
    pieces, far, where = gather_weight(
        slabs, out_weight.shape[0], place, sent[:1], ()
    )
    grad_attn = grad_attn_rows(where, lengths, after(grad_out[0], *slots[1:]), pieces, far)

    own = (queries[0], own_keys[0], own_values[0])
    results, backs = (), []
    for part in PARTS:
        out = attend(meta, *own, grad_attn, slots, ids.shape[0], part, results)
        results, back = out[:4], out[4:]
        backs.append([back[0]] + [move(back[j], 1, -j) for j in range(1, 4)])
    attn_t, *grads = results
    total = grad_weight_rows(after(attn_t, *backs[0][1:]), grad_out[0])
    own, opposite, near = begin_sum(total, "z")
    sums = fold_rows(table, backs)
    total = end_sum(after(own, sums[0]), opposite, near, "z")
    total = end_sum(*begin_sum(total, "x"), "x")
    attended = attended_rows(where, after(attn_t, total), pieces, far)
    grad_weight = end_sum(*begin_sum(total, "y"), "y")
    mine = after(sums[0], attended)
    grad_cache = total_rows([mine] + [move(sums[k], 0, -k) for k in range(1, 4)])
    return (attended[None], *(grad[None] for grad in grads), grad_cache, grad_weight)


def solution(mesh):
    axes = ("z", "core", "x", "y")
    fine = Mesh(mesh.devices.reshape(4, 2, 4, 4), axes)

    def split(rank):
        return P(axes, *([None] * (rank - 1)))

    return jax.shard_map(
        body,
        mesh=fine,
        in_specs=tuple(split(rank) for rank in (3, 3, 3, 1, 2, 4, 2, 3)),
        out_specs=tuple(split(rank) for rank in (3, 3, 3, 3, 4, 2)),
        check_vma=False,
    )
```

```python
import functools

import jax
import jax.numpy as jnp
from jax import lax
from jax.experimental import pallas as pl
from jax.experimental.pallas import tpu as pltpu
from jax.sharding import Mesh
from jax.sharding import PartitionSpec as P

HD = 64
BLK = 64
LANES = 128
LOG2E = 1.4426950408889634
BF = jnp.bfloat16
F32 = jnp.float32
MIB = 1024 * 1024
PARTS = ((0, 512), (512, 768))
STEP = 2 * LANES
PLANE = ("core", "x", "y")


def shift(array, axis, amount):
    n = lax.axis_size(axis)
    return lax.ppermute(array, axis, [(i, (i + amount) % n) for i in range(n)])


def move(array, leg, amount):
    pairs = []
    for core in range(2):
        for x in range(4):
            for y in range(4):
                along_x = (leg == 0) == (core == 0)
                to_x, to_y = ((x + amount) % 4, y) if along_x else (x, (y + amount) % 4)
                pairs.append((core * 16 + x * 4 + y, core * 16 + to_x * 4 + to_y))
    return lax.ppermute(array, PLANE, pairs)


def cost(us):
    return pl.CostEstimate(flops=int(us * 1.15e9), bytes_accessed=0, transcendentals=0)


def after(array, *earlier):
    return lax.optimization_barrier((array, earlier))[0]


def nt(a, b):
    return lax.dot_general(a, b, (((1,), (1,)), ((), ())), preferred_element_type=F32)


def mm(a, b):
    return lax.dot_general(a, b, (((1,), (0,)), ((), ())), preferred_element_type=F32)


def select_kernel(table, *refs):
    held, out = refs[:4], refs[4:]
    for j in range(4):
        for k in range(4):
            row = jnp.maximum(table[j * 4 + k], 0)
            out[j][k] = held[k][row]


def select_rows(table, held):
    _, kinds, rows, width = held[0].shape
    block_in = pl.BlockSpec((2, kinds, rows, STEP), lambda i, t: (0, 0, 0, i))
    block_out = pl.BlockSpec((4, kinds, rows, STEP), lambda i, t: (0, 0, 0, i))
    return pl.pallas_call(
        select_kernel,
        grid_spec=pltpu.PrefetchScalarGridSpec(
            num_scalar_prefetch=1,
            grid=(width // STEP,),
            in_specs=[block_in] * 4,
            out_specs=[block_out] * 4,
        ),
        out_shape=[jax.ShapeDtypeStruct((4, kinds, rows, width), BF)] * 4,
        compiler_params=pltpu.CompilerParams(vmem_limit_bytes=12 * MIB),
        cost_estimate=cost(3),
        name="select_rows",
    )(table.reshape(-1), *held)


def fold_kernel(table, *refs):
    out = refs[-4:]
    step = pl.program_id(0)
    for number, (start, width) in enumerate(PARTS):
        parts = refs[4 * number : 4 * number + 4]

        @pl.when((step >= start // STEP) & (step < (start + width) // STEP))
        def _():
            for k in range(4):
                for row in range(2):
                    total = None
                    for j in range(4):
                        keep = jnp.where(table[j * 4 + k] == row, 1.0, 0.0).astype(F32)
                        term = parts[j][k].astype(F32) * keep
                        total = term if total is None else total + term
                    out[k][row] = total.astype(BF)


def fold_rows(table, backs):
    _, kinds, rows, _ = backs[0][0].shape
    columns = sum(width for _, width in PARTS)
    blocks = []
    for start, width in PARTS:
        first, last = start // STEP, width // STEP - 1
        blocks += [
            pl.BlockSpec(
                (4, kinds, rows, STEP),
                lambda i, t, first=first, last=last: (0, 0, 0, jnp.clip(i - first, 0, last)),
            )
        ] * 4
    return pl.pallas_call(
        fold_kernel,
        grid_spec=pltpu.PrefetchScalarGridSpec(
            num_scalar_prefetch=1,
            grid=(columns // STEP,),
            in_specs=blocks,
            out_specs=[pl.BlockSpec((2, kinds, rows, STEP), lambda i, t: (0, 0, 0, i))] * 4,
        ),
        out_shape=[jax.ShapeDtypeStruct((2, kinds, rows, columns), BF)] * 4,
        compiler_params=pltpu.CompilerParams(vmem_limit_bytes=58 * MIB),
        cost_estimate=cost(4),
        name="fold_rows",
    )(table.reshape(-1), *backs[0], *backs[1])


def total_kernel(*refs):
    total = refs[0][...].astype(F32)
    for part in refs[1:-1]:
        total = total + part[...].astype(F32)
    refs[-1][...] = total


def total_rows(parts):
    owned, kinds, rows, width = parts[0].shape
    block = pl.BlockSpec((owned, kinds, rows, STEP), lambda i: (0, 0, 0, i))
    return pl.pallas_call(
        total_kernel,
        grid=(width // STEP,),
        in_specs=[block] * 4,
        out_specs=block,
        out_shape=jax.ShapeDtypeStruct((owned, kinds, rows, width), F32),
        compiler_params=pltpu.CompilerParams(vmem_limit_bytes=12 * MIB),
        cost_estimate=cost(4),
        name="total_rows",
    )(*parts)


def head_front(keys, values, query, grad_t, head):
    lane = lax.broadcasted_iota(jnp.int32, query.shape, 1) // HD
    feature = lax.broadcasted_iota(jnp.int32, grad_t.shape, 0) // HD
    query = jnp.where(lane == head, query, jnp.zeros_like(query))
    grad_t = jnp.where(feature == head, grad_t, jnp.zeros_like(grad_t))
    return query, grad_t, nt(keys, query), mm(values, grad_t)


def head_softmax(scores, grad_probs, valid_frames):
    frames = scores.shape[1]
    key_row = lax.broadcasted_iota(jnp.int32, (frames, frames), 0)
    own = jnp.where(key_row < valid_frames, scores[:frames], -1e30)
    scores = jnp.concatenate([own, scores[frames:]], 0)
    top = jnp.max(scores, axis=0, keepdims=True)
    expo = jnp.exp2((scores - top) * (HD**-0.5 * LOG2E))
    probs = expo * (1.0 / jnp.sum(expo, axis=0, keepdims=True))
    row_dots = jnp.sum(probs * grad_probs, axis=0, keepdims=True)
    return probs.astype(BF), (probs * (grad_probs - row_dots)).astype(BF)


def attend_kernel(meta, q_ref, ko_ref, vo_ref, g_ref, *refs):
    slots = refs[:4]
    attn_t_ref, dq_ref, dk_ref, dv_ref = refs[-12:-8]
    back, (k_all, v_all, dk_all, dv_all) = refs[-8:-4], refs[-4:]
    frames, width = q_ref.shape
    scale = HD**-0.5
    valid_frames = meta[16] * BLK
    k_all[:frames] = ko_ref[...]
    v_all[:frames] = vo_ref[...]

    def rows_of(place):
        return pl.ds(pl.multiple_of(frames + BLK * jnp.maximum(place, 0), BLK), BLK)

    for j in range(4):
        for k in range(4):
            place = meta[4 * j + k]

            @pl.when(place >= 0)
            def _():
                k_all[rows_of(place)] = slots[j][k, 0]
                v_all[rows_of(place)] = slots[j][k, 1]

    for pair in range(width // LANES):
        lanes = slice(pair * LANES, (pair + 1) * LANES)
        keys, values = k_all[:, lanes], v_all[:, lanes]
        keys_t, values_t = keys.T, values.T
        fronts = [head_front(keys, values, q_ref[:, lanes], g_ref[lanes], h) for h in range(2)]
        outs_t, dqs_t, dks, dvs = [], [], [], []
        for h, (query, grad_t, scores, grad_probs) in enumerate(fronts):
            probs, grad_scores = head_softmax(scores, grad_probs, valid_frames)
            mine = slice(h * HD, (h + 1) * HD)
            outs_t.append(mm(values_t[mine], probs))
            dqs_t.append(mm(keys_t[mine], grad_scores))
            dks.append(mm(grad_scores, query))
            dvs.append(nt(probs, grad_t))
        out_t = jnp.concatenate(outs_t, 0)
        column = lax.broadcasted_iota(jnp.int32, out_t.shape, 1)
        attn_t_ref[lanes] = jnp.where(column < valid_frames, out_t, 0.0).astype(BF)
        dq_ref[:, lanes] = (jnp.concatenate(dqs_t, 0) * scale).T.astype(BF)
        grad_key = ((dks[0] + dks[1]) * scale).astype(BF)
        grad_value = (dvs[0] + dvs[1]).astype(BF)
        dk_ref[:, lanes] = grad_key[:frames]
        dv_ref[:, lanes] = grad_value[:frames]
        dk_all[:, lanes] = grad_key[frames:]
        dv_all[:, lanes] = grad_value[frames:]

    for j in range(4):
        for k in range(4):
            place = meta[4 * j + k]
            rows = pl.ds(pl.multiple_of(BLK * jnp.maximum(place, 0), BLK), BLK)

            @pl.when(place >= 0)
            def _():
                back[j][k, 0] = dk_all[rows]
                back[j][k, 1] = dv_all[rows]

            @pl.when(place < 0)
            def _():
                back[j][k] = jnp.zeros(back[j].shape[1:], BF)


def attend(meta, query, own_keys, own_values, grad_attn, slots, entries, part, kept):
    frames, features = query.shape
    first = part[0] // STEP
    wide = pl.BlockSpec((frames, STEP), lambda i, m: (0, first + i))
    tall = pl.BlockSpec((STEP, frames), lambda i, m: (first + i, 0))
    slot = pl.BlockSpec((4, 2, BLK, STEP), lambda i, m: (0, 0, 0, first + i))
    back = pl.BlockSpec((4, 2, BLK, STEP), lambda i, m: (0, 0, 0, i))
    keys, blocks = frames + entries * BLK, entries * BLK
    rows = jax.ShapeDtypeStruct((frames, features), BF)
    return pl.pallas_call(
        attend_kernel,
        grid_spec=pltpu.PrefetchScalarGridSpec(
            num_scalar_prefetch=1,
            grid=(part[1] // STEP,),
            in_specs=[wide] * 3 + [tall] + [slot] * 4
            + [pl.BlockSpec(memory_space=pl.ANY)] * len(kept),
            out_specs=[tall] + [wide] * 3 + [back] * 4,
            scratch_shapes=[pltpu.VMEM((keys, STEP), BF)] * 2
            + [pltpu.VMEM((blocks, STEP), BF)] * 2,
        ),
        out_shape=[jax.ShapeDtypeStruct((features, frames), BF)]
        + [rows] * 3
        + [jax.ShapeDtypeStruct((4, 2, BLK, part[1]), BF)] * 4,
        input_output_aliases={9 + i: i for i in range(len(kept))},
        compiler_params=pltpu.CompilerParams(vmem_limit_bytes=58 * MIB),
        cost_estimate=cost(part[1] // STEP * 4.6),
        name="attend",
    )(meta, query, own_keys, own_values, grad_attn, *slots, *kept)


def spread_slab(rows, ids):
    size, features = rows.shape
    note = jnp.pad(ids.astype(BF), (0, features - ids.shape[0]))[None]
    slab = jnp.concatenate([rows, note, jnp.zeros((15 - size, features), BF)], 0)
    return jnp.stack([slab] + [move(slab, 1, k) for k in range(1, 4)])


def gather_weight(slabs, size, place, before_z, before_core):
    z, core = lax.axis_index("z"), lax.axis_index("core")
    features = slabs[0].shape[-1]
    row = jnp.arange(16, dtype=jnp.int32)
    target = jnp.where(row < size, place.reshape(16, 1) * size + row, -1).reshape(1, 256)
    pick = (jnp.arange(16 * size, dtype=jnp.int32)[:, None] == target).astype(BF)
    rows = mm(pick, jnp.concatenate(slabs, 0).reshape(256, features)).astype(BF)
    rows = after(rows, *before_z)
    pieces = [rows] + [shift(rows, "z", k) for k in range(1, 4)]
    far = [shift(piece, "core", 1) for piece in pieces]
    from_z = (z - jnp.arange(4, dtype=jnp.int32)) % 4
    return pieces, far, jnp.concatenate([from_z * 2 + core, from_z * 2 + 1 - core])


def grad_attn_kernel(meta, grad_ref, *refs):
    pieces, out = refs[:8], refs[8]
    size, frames = pieces[0].shape[0], grad_ref.shape[0]
    column = lax.broadcasted_iota(jnp.int32, (size, frames), 1)
    for i, piece in enumerate(pieces):
        part = jnp.where(column < meta[8] * BLK, nt(piece[...], grad_ref[...]), 0.0)
        out[pl.ds(pl.multiple_of(meta[i] * size, 32), size)] = part.astype(BF)


def grad_attn_rows(where, lengths, grad_rows, pieces, far):
    frames, features = grad_rows.shape
    return pl.pallas_call(
        grad_attn_kernel,
        in_specs=[pl.BlockSpec(memory_space=pltpu.SMEM)]
        + [pl.BlockSpec(memory_space=pltpu.VMEM)] * 9,
        out_specs=pl.BlockSpec(memory_space=pltpu.VMEM),
        out_shape=jax.ShapeDtypeStruct((features, frames), BF),
        compiler_params=pltpu.CompilerParams(vmem_limit_bytes=12 * MIB),
        cost_estimate=cost(4),
        name="grad_attn",
    )(jnp.concatenate([where, lengths]), grad_rows, *pieces, *far)


def attended_kernel(where, attn_t_ref, *refs):
    pieces, out = refs[:8], refs[8]
    size = pieces[0].shape[0]
    total = None
    for i, piece in enumerate(pieces):
        rows = attn_t_ref[pl.ds(pl.multiple_of(where[i] * size, 32), size)]
        part = mm(rows.T, piece[...])
        total = part if total is None else total + part
    out[...] = total.astype(BF)


def attended_rows(where, attn_t, pieces, far):
    features, frames = attn_t.shape
    wide = 2 * LANES
    size = features // 8
    return pl.pallas_call(
        attended_kernel,
        grid_spec=pltpu.PrefetchScalarGridSpec(
            num_scalar_prefetch=1,
            grid=(features // wide,),
            in_specs=[pl.BlockSpec((features, frames), lambda i, w: (0, 0))]
            + [pl.BlockSpec((size, wide), lambda i, w: (0, i))] * 8,
            out_specs=pl.BlockSpec((frames, wide), lambda i, w: (0, i)),
        ),
        out_shape=jax.ShapeDtypeStruct((frames, features), BF),
        compiler_params=pltpu.CompilerParams(vmem_limit_bytes=58 * MIB),
        cost_estimate=cost(0.1),
        name="attended",
    )(where, attn_t, *pieces, *far)


def grad_weight_kernel(core, attn_t_ref, grad_ref, out_ref):
    out_ref[0] = mm(attn_t_ref[...], grad_ref[...]).astype(out_ref.dtype)


def grad_weight_half(core, attn_t, grad_rows, dtype):
    features, frames = attn_t.shape
    size = features // 8
    return pl.pallas_call(
        grad_weight_kernel,
        grid_spec=pltpu.PrefetchScalarGridSpec(
            num_scalar_prefetch=1,
            grid=(4,),
            in_specs=[
                pl.BlockSpec((size, frames), lambda i, c: (2 * i + c[0], 0)),
                pl.BlockSpec((frames, features), lambda i, c: (0, 0)),
            ],
            out_specs=pl.BlockSpec((1, size, features), lambda i, c: (i, 0, 0)),
        ),
        out_shape=jax.ShapeDtypeStruct((4, size, features), dtype),
        compiler_params=pltpu.CompilerParams(vmem_limit_bytes=58 * MIB),
        cost_estimate=cost(0.1),
        name="grad_weight",
    )(core.reshape(1).astype(jnp.int32), attn_t, grad_rows)


def grad_weight_rows(attn_t, grad_rows):
    core = lax.axis_index("core")
    far = grad_weight_half(1 - core, attn_t, grad_rows, BF)
    near = grad_weight_half(core, attn_t, grad_rows, F32)
    total = near + shift(far, "core", 1).astype(F32)
    return total.reshape(-1, grad_rows.shape[1])


def begin_sum(total, axis):
    me = lax.axis_index(axis)
    rows = total.shape[0] // 4
    pieces = [lax.dynamic_slice_in_dim(total, (me + k) % 4 * rows, rows, 0) for k in range(4)]
    return pieces[0], pieces[2].astype(BF), [shift(pieces[k].astype(BF), axis, k) for k in (1, 3)]


def end_sum(own, opposite, near, axis):
    for piece in (*near, shift(opposite, axis, 2)):
        own = own + piece.astype(F32)
    return own


def body(queries, own_keys, own_values, lengths, history, cache_blocks, out_weight, grad_out):
    owned = cache_blocks.shape[0]
    x, y, core = (lax.axis_index(axis) for axis in ("x", "y", "core"))
    straight = core == 0
    first, second = jnp.where(straight, x, y), jnp.where(straight, y, x)
    steps = jnp.arange(4, dtype=jnp.int32)
    ids = history[0]
    owners = ids // owned
    owner_x, owner_y = owners // 4, owners % 4
    behind_first = (first - jnp.where(straight, owner_x, owner_y)) % 4
    behind_second = (second - jnp.where(straight, owner_y, owner_x)) % 4
    slot = behind_second * 4 + behind_first
    every = jnp.arange(16, dtype=jnp.int32)[:, None]
    rank = jnp.sum((slot[None, :] < every).astype(jnp.int32), axis=1)
    rank = jnp.where(jnp.any(slot[None, :] == every, axis=1), rank, -1)
    meta = jnp.concatenate([rank, lengths]).astype(jnp.int32)

    slab = spread_slab(out_weight, ids)
    note = slab[:, out_weight.shape[0], : ids.shape[0]].astype(jnp.int32)
    asked = jnp.stack([ids] + [note[4 - j] for j in range(1, 4)])
    along_first, along_second = (first - steps) % 4, (second - steps) % 4
    owner = jnp.where(straight, along_first * 4 + second, second * 4 + along_first)
    match = (asked // owned)[:, None, :] == owner[None, :, None]
    table = jnp.max(jnp.where(match, (asked % owned)[:, None, :], -1), axis=2)

    held = [cache_blocks] + [move(cache_blocks, 0, k) for k in range(1, 4)]
    sent = select_rows(table, held)
    slots = [sent[0]] + [move(sent[j], 1, j) for j in range(1, 4)]

    place = jnp.where(
        straight,
        along_first[:, None] * 4 + along_second[None, :],
        along_second[None, :] * 4 + along_first[:, None],
    )
    slab = after(slab, held[1])
    slabs = [slab] + [move(slab, 0, k) for k in range(1, 4)]
    pieces, far, where = gather_weight(
        slabs, out_weight.shape[0], place, sent[:1], ()
    )
    grad_attn = grad_attn_rows(where, lengths, after(grad_out[0], *slots[1:]), pieces, far)

    own = (queries[0], own_keys[0], own_values[0])
    results, backs = (), []
    for part in PARTS:
        out = attend(meta, *own, grad_attn, slots, ids.shape[0], part, results)
        results, back = out[:4], out[4:]
        backs.append([back[0]] + [move(back[j], 1, -j) for j in range(1, 4)])
    attn_t, *grads = results
    total = grad_weight_rows(after(attn_t, *backs[0][1:]), grad_out[0])
    own, opposite, near = begin_sum(total, "z")
    sums = fold_rows(table, backs)
    total = end_sum(after(own, sums[0]), opposite, near, "z")
    total = end_sum(*begin_sum(total, "x"), "x")
    attended = attended_rows(where, after(attn_t, total), pieces, far)
    grad_weight = end_sum(*begin_sum(total, "y"), "y")
    mine = after(sums[0], attended)
    grad_cache = total_rows([mine] + [move(sums[k], 0, -k) for k in range(1, 4)])
    return (attended[None], *(grad[None] for grad in grads), grad_cache, grad_weight)


def solution(mesh):
    axes = ("z", "core", "x", "y")
    fine = Mesh(mesh.devices.reshape(4, 2, 4, 4), axes)

    def split(rank):
        return P(axes, *([None] * (rank - 1)))

    return jax.shard_map(
        body,
        mesh=fine,
        in_specs=tuple(split(rank) for rank in (3, 3, 3, 1, 2, 4, 2, 3)),
        out_specs=tuple(split(rank) for rank in (3, 3, 3, 3, 4, 2)),
        check_vma=False,
    )
```
